32 devices in a mesh: batch: 16 (over z, x, core), rank: 2 (over y).
Axes of the slice: x: 2, y: 2, z: 4, core: 2. Of those that a mesh axis runs over, the one named last changes fastest.
Arguments:
- tokens: bfloat16 [16384, 768], P('batch'), may hold values from -6 to 6
- valid_len: int32 [32], P('batch'), may hold values from 128 to 512, as said below
- w_query: bfloat16 [2, 768, 768], P(None, None, 'rank'), may hold values from -0.21875 to 0.21875
- w_key: bfloat16 [2, 768, 768], P(None, None, 'rank'), may hold values from -0.21875 to 0.21875
- w_value: bfloat16 [2, 768, 768], P(None, None, 'rank'), may hold values from -0.21875 to 0.21875
- w_out: bfloat16 [2, 768, 768], P(None, 'rank'), may hold values from -0.875 to 0.875
- w_up: bfloat16 [2, 768, 3072], P(None, None, 'rank'), may hold values from -0.21875 to 0.21875
- w_down: bfloat16 [2, 3072, 768], P(None, 'rank'), may hold values from -0.109375 to 0.109375
- mat_a: bfloat16 [768, 1024], P(None, 'rank'), may hold values from -0.21875 to 0.21875
- mat_b: bfloat16 [1024, 768], P('rank'), may hold values from -0.1875 to 0.1875
- scale_dq: float32 [2, 1024], P(None, 'rank'), may hold values from 0.25 to 2
- scale_bq: float32 [2, 768], P(None, 'rank'), may hold values from -3 to 3
- scale_dv: float32 [2, 1024], P(None, 'rank'), may hold values from 0.25 to 2
- scale_bv: float32 [2, 768], P(None, 'rank'), may hold values from -3 to 3
- cotangent: bfloat16 [16384, 768], P('batch'), may hold values from -6 to 6
Outputs:
- output: float32 [16384, 768], P('batch')
- grad_tokens: float32 [16384, 768], P('batch')
- grad_dq: float32 [2, 1024], P(None, 'rank')
- grad_bq: float32 [2, 768], P(None, 'rank')
- grad_dv: float32 [2, 1024], P(None, 'rank')
- grad_bv: float32 [2, 768], P(None, 'rank')
The draws below stay inside these ranges and needn't reach their ends.
Inputs may be any that keep to these rules, and one draw needn't show every extreme that they name: valid_len[p] is the number of leading slots of pair p that hold tokens; at least one pair holds 512.
All inputs are finite; a program needn't handle non-finite values.
Results may differ from the reference program's by a relative error of at most 0.024.
Values may be sent and summed in bfloat16 or wider, within the bound.
A program may use at most 192 MiB of HBM per device.

```python
import math
import jax
import jax.numpy as jnp
from jax import lax

D = 768
HEADS = 12
HEAD_DIM = 64
FF = 3072
VERA_RANK = 1024
SEQ = 512
LAYERS = 2
PAIRS = 32
TOKENS = 16384


def draw_valid_len(key, part):
    key = jax.random.fold_in(key, 11)
    first_key, second_key = jax.random.split(key)
    lengths = jax.random.randint(first_key, (PAIRS,), SEQ // 4, SEQ + 1)
    chosen = jax.random.randint(second_key, (), 0, PAIRS)
    return jnp.where(jnp.arange(PAIRS) == chosen, SEQ, lengths).astype(jnp.int32)


def level_of(stream_key, dims, cuts, low, high):
    loudness, own = 1.0, jax.random.fold_in(stream_key, 6)
    for axis_at, shards_of in cuts:
        draws = jnp.exp(jax.random.uniform(jax.random.fold_in(own, axis_at), (shards_of,), jnp.float32, low / len(cuts), high / len(cuts)))
        loudness = loudness * jnp.repeat(draws, dims[axis_at] // shards_of).reshape([-1 if axis == axis_at else 1 for axis in range(len(dims))])
    return loudness


def centred(own_key, extent, scale, reach, cuts=(), kind=jnp.bfloat16):
    entries = scale * jax.random.normal(own_key, extent, jnp.float32)
    if cuts:
        entries = entries * level_of(own_key, extent, cuts, -0.22, 0.18)
    return jnp.clip(entries, -reach, reach).astype(kind)


def setup_inputs(seed: int = 0) -> dict:
    streams_of = jax.random.split(jax.random.key(seed), 16)
    tokens = centred(streams_of[0], (TOKENS, D), 1.0, 6.0, ((0, 16),))
    valid_len = draw_valid_len(jax.random.fold_in(streams_of[15], 71), 0)
    w_query = centred(streams_of[2], (LAYERS, D, D), D ** -0.5, 0.21875, ((2, 2),))
    w_key = centred(streams_of[3], (LAYERS, D, D), D ** -0.5, 0.21875, ((2, 2),))
    w_value = centred(streams_of[4], (LAYERS, D, D), D ** -0.5, 0.21875, ((2, 2),))
    w_out = centred(streams_of[5], (LAYERS, D, D), (D // 16) ** -0.5, 0.875, ((1, 2),))
    w_up = centred(streams_of[6], (LAYERS, D, FF), D ** -0.5, 0.21875, ((2, 2),))
    w_down = centred(streams_of[7], (LAYERS, FF, D), FF ** -0.5, 0.109375, ((1, 2),))
    mat_a = centred(streams_of[8], (D, VERA_RANK), D ** -0.5, 0.21875, ((1, 2),))
    mat_b = centred(streams_of[9], (VERA_RANK, D), VERA_RANK ** -0.5, 0.1875, ((0, 2),))
    scale_dq = jnp.clip(jnp.exp(math.log(2.0) - 2.0794415 * jax.random.uniform(streams_of[10], (LAYERS, VERA_RANK), jnp.float32) ** level_of(streams_of[10], (LAYERS, VERA_RANK), ((1, 2),), -0.2, 0.2)), 0.25, 2.0)
    scale_bq = centred(streams_of[11], (LAYERS, D), 0.5, 3.0, ((1, 2),), jnp.float32)
    scale_dv = jnp.clip(jnp.exp(math.log(2.0) - 2.0794415 * jax.random.uniform(streams_of[12], (LAYERS, VERA_RANK), jnp.float32) ** level_of(streams_of[12], (LAYERS, VERA_RANK), ((1, 2),), -0.2, 0.2)), 0.25, 2.0)
    scale_bv = centred(streams_of[13], (LAYERS, D), 0.5, 3.0, ((1, 2),), jnp.float32)
    cotangent = centred(streams_of[14], (TOKENS, D), 1.0, 6.0, ((0, 16),))
    return dict(tokens=tokens, valid_len=valid_len, w_query=w_query, w_key=w_key, w_value=w_value, w_out=w_out, w_up=w_up, w_down=w_down, mat_a=mat_a, mat_b=mat_b, scale_dq=scale_dq, scale_bq=scale_bq, scale_dv=scale_dv, scale_bv=scale_bv, cotangent=cotangent)


@jax.custom_vjp
def low(v):
    return lax.optimization_barrier(v.astype(jnp.bfloat16)).astype(jnp.float32)

@jax.custom_vjp
def low_back(v):
    return v

def low_keep(v):
    return (low(v), None)

def low_pass(kept, grad):
    return (grad,)

def back_keep(v):
    return (v, None)

def back_low(kept, grad):
    return (low(grad),)
low.defvjp(low_keep, low_pass)
low_back.defvjp(back_keep, back_low)
masked = -1e+30

def rounded(values):
    return low_back(low(values))

def project(operand, matrix):
    return jnp.einsum('...d,de->...e', operand, matrix, precision=lax.Precision.HIGHEST)

def normalize(values):
    center = values - lax.optimization_barrier(jnp.mean(values, axis=-1, keepdims=True))
    spread = lax.optimization_barrier(jnp.mean(center * center, axis=-1, keepdims=True))
    return center * lax.rsqrt(spread + 1e-05)

def layer_model(inputs, key_mask, w_query, w_key, w_value, w_out, w_up, w_down, mat_a, mat_b, scale_dq, scale_bq, scale_dv, scale_bv):
    group_count, seq_len, model_width = inputs.shape
    rows_low = low(inputs)
    inner = low_back(project(rows_low, mat_a))
    lift_query = low_back(project(low(inner * scale_dq), mat_b))
    lift_value = low_back(project(low(inner * scale_dv), mat_b))
    query_rows = rounded(project(rows_low, w_query) + lift_query * scale_bq)
    key_rows = rounded(project(rows_low, w_key))
    value_rows = rounded(project(rows_low, w_value) + lift_value * scale_bv)

    def to_heads(rows):
        return rows.reshape(group_count, seq_len, HEADS, HEAD_DIM)
    scores = jnp.einsum('gqhe,gkhe->ghqk', to_heads(query_rows), to_heads(key_rows), precision=lax.Precision.HIGHEST) * HEAD_DIM ** (-0.5)
    scores = low_back(jnp.where(key_mask[:, None, None, :], scores, masked))
    row_peak = lax.optimization_barrier(jnp.max(scores, axis=-1, keepdims=True))
    exponent = jnp.exp(scores - row_peak)
    weights_low = low(exponent / lax.optimization_barrier(jnp.sum(exponent, axis=-1, keepdims=True)))
    attended = jnp.einsum('ghqk,gkhe->gqhe', weights_low, to_heads(value_rows), precision=lax.Precision.HIGHEST)
    attended = rounded(attended.reshape(group_count, seq_len, model_width))
    first_sum = inputs + low_back(project(attended, w_out))
    normed = normalize(first_sum)
    before = low_back(project(low(normed), w_up))
    hidden = low(jax.nn.gelu(before, approximate=False))
    second_sum = normed + low_back(project(hidden, w_down))
    return normalize(second_sum)

def reference(tokens, valid_len, w_query, w_key, w_value, w_out, w_up, w_down, mat_a, mat_b, scale_dq, scale_bq, scale_dv, scale_bv, cotangent):
    frozen = tuple((weight.astype(jnp.float32) for weight in (w_query, w_key, w_value, w_out, w_up, w_down)))
    shared_a = mat_a.astype(jnp.float32)
    shared_b = mat_b.astype(jnp.float32)
    group_size = math.gcd(PAIRS, 4)
    block_count = PAIRS // group_size
    token_rows = tokens.astype(jnp.float32).reshape(block_count, group_size, SEQ, D)
    upstream = cotangent.astype(jnp.float32).reshape(block_count, group_size, SEQ, D)
    key_masks = (jnp.arange(SEQ, dtype=jnp.int32)[None, :] < valid_len[:, None]).reshape(block_count, group_size, SEQ)

    def block_step(running, pieces):
        inputs, key_mask, incoming = pieces

        def network(hidden_rows, vec_dq, vec_bq, vec_dv, vec_bv):
            for level_index in range(LAYERS):
                hidden_rows = layer_model(hidden_rows, key_mask, frozen[0][level_index], frozen[1][level_index], frozen[2][level_index], frozen[3][level_index], frozen[4][level_index], frozen[5][level_index], shared_a, shared_b, vec_dq[level_index], vec_bq[level_index], vec_dv[level_index], vec_bv[level_index])
            return hidden_rows
        outputs, pull_back = jax.vjp(network, inputs, scale_dq, scale_bq, scale_dv, scale_bv)
        gradients = pull_back(incoming)
        running = tuple((total_sum + part_sum for total_sum, part_sum in zip(running, gradients[1:])))
        return (running, (outputs, gradients[0]))
    initial = tuple((jnp.zeros(vector.shape, jnp.float32) for vector in (scale_dq, scale_bq, scale_dv, scale_bv)))
    totals, (outputs, grad_in) = lax.scan(block_step, initial, (token_rows, key_masks, upstream))
    return (outputs.reshape(TOKENS, D), grad_in.reshape(TOKENS, D), totals[0], totals[1], totals[2], totals[3])
```

```python
import functools

import jax
import jax.numpy as jnp
from jax import lax
from jax.experimental import pallas as pl
from jax.experimental.pallas import tpu as pltpu
from jax.sharding import PartitionSpec as P

HEAD_DIM = 64
MESH = pl.DeviceIdType.MESH

epsilon = 1e-05
masked = -1e30


def flip(index, bit):
    step = 1 << bit
    return index + step - 2 * step * ((index // step) % 2)


class Exchange:
    LAG = 4
    HOP = 2

    def __init__(self, groups, loads, sems):
        self.groups, self.loads = groups, loads
        self.y_send, self.y_recv, self.x_send, self.x_recv, self.z_send, self.z_recv, self.c_send, self.c_recv = sems
        self.batch = lax.axis_index("batch")
        self.rank = lax.axis_index("rank")
        b = self.batch
        self.core = b % 2
        bit_x, bit_z = (b // 2) % 2, (b // 4) % 2
        self.partner = {
            "y": (b, 1 - self.rank),
            "x": (flip(b, 1), self.rank),
            "z": (flip(b, 2), self.rank),
            "c": (flip(b, 0), self.rank),
        }
        chip = lambda cx, cz: cx + 2 * cz
        own, across, along, far = (
            chip(bit_x, bit_z),
            chip(1 - bit_x, bit_z),
            chip(bit_x, 1 - bit_z),
            chip(1 - bit_x, 1 - bit_z),
        )
        parity = (bit_x + bit_z) % 2
        first = lambda who: 2 * who
        second = lambda who: 2 * who + 1
        pair = lambda par, which: 8 + 2 * par + which
        self.y_units = [first(own), second(own), pair(parity, 0), pair(parity, 1)]
        self.x_units = [first(across), second(across), pair(1 - parity, 0), second(far)]
        self.z_units = [first(along), second(along), first(far), pair(1 - parity, 1)]
        self.x_out = [first(own), second(own), pair(parity, 0), second(along)]
        self.z_out = [first(own), second(own), first(across), pair(parity, 1)]
        self.count = 4 * len(groups)
        self.pending = []
        self.next_tick = 0
        self.plan()

    def barrier(self):
        bar = pltpu.get_barrier_semaphore()
        for who in self.partner.values():
            pl.semaphore_signal(bar, inc=1, device_id=who, device_id_type=MESH)
        pl.semaphore_wait(bar, len(self.partner))

    def copy(self, src, dst, send, recv, link):
        return pltpu.make_async_remote_copy(
            src_ref=src, dst_ref=dst, send_sem=send, recv_sem=recv,
            device_id=self.partner[link], device_id_type=MESH,
        )

    def full(self, group, unit, core, rank):
        return self.groups[group](2 * unit + core, rank)

    def y_copy(self, item):
        g, j = divmod(item, 4)
        ref = self.full(g, self.y_units[j], self.core, self.rank)
        return self.copy(ref, ref, self.y_send.at[item], self.y_recv.at[item], "y")

    def plane_copy(self, item, link):
        g, j = divmod(item, 4)
        unit = (self.x_out if link == "x" else self.z_out)[j]
        send, recv = (self.x_send, self.x_recv) if link == "x" else (self.z_send, self.z_recv)
        ref = self.full(g, unit, self.core, 1 - self.rank)
        return self.copy(ref, ref, send.at[item], recv.at[item], link)

    def core_copy(self, item, link):
        g, j = divmod(item, 4)
        unit = {"y": self.y_units, "x": self.x_units, "z": self.z_units}[link][j]
        slot = 3 * item + {"y": 0, "x": 1, "z": 2}[link]
        ref = self.full(g, unit, self.core, 1 - self.rank)
        return self.copy(ref, ref, self.c_send.at[slot], self.c_recv.at[slot], "c")

    def core_arrival(self, item, link):
        g, j = divmod(item, 4)
        unit = {"y": self.y_units, "x": self.x_units, "z": self.z_units}[link][j]
        slot = 3 * item + {"y": 0, "x": 1, "z": 2}[link]
        ref = self.full(g, unit, 1 - self.core, 1 - self.rank)
        return self.copy(ref, ref, self.c_send.at[slot], self.c_recv.at[slot], "c")

    def y_arrival(self, item):
        g, j = divmod(item, 4)
        ref = self.full(g, self.y_units[j], self.core, 1 - self.rank)
        return self.copy(ref, ref, self.y_send.at[item], self.y_recv.at[item], "y")

    def plane_arrival(self, item, link):
        g, j = divmod(item, 4)
        unit = (self.x_units if link == "x" else self.z_units)[j]
        send, recv = (self.x_send, self.x_recv) if link == "x" else (self.z_send, self.z_recv)
        ref = self.full(g, unit, self.core, 1 - self.rank)
        return self.copy(ref, ref, send.at[item], recv.at[item], link)

    def plan(self):
        lag, hop = self.LAG, self.HOP
        begin = {}
        for item in range(self.count):
            begin["y", item] = item
        for group in range(self.count // 4):
            at = lambda link, j: begin[link, 4 * group + j] + lag
            for link, j in (("x", 0), ("x", 1), ("x", 2), ("z", 0), ("z", 1), ("z", 3)):
                begin[link, 4 * group + j] = at("y", j)
            begin["z", 4 * group + 2] = at("x", 0)
            begin["x", 4 * group + 3] = at("z", 1)
        steps = {}
        order = {"y": 0, "x": 1, "z": 2}
        for (link, item), tick in begin.items():
            arrived = tick + lag
            steps.setdefault(tick, []).append((1, order[link], item, "send", link))
            steps.setdefault(arrived, []).append((0, order[link], item, "arrive", link))
            steps.setdefault(arrived, []).append((2, order[link], item, "share", link))
            steps.setdefault(arrived + hop, []).append((3, order[link], item, "shared", link))
            steps.setdefault(arrived + lag, []).append((4, order[link], item, "sent", link))
        self.steps = {tick: sorted(found) for tick, found in steps.items()}
        self.last_tick = max(steps)
        self.ready = {}
        for tick, found in steps.items():
            for entry in found:
                if entry[3] == "shared":
                    group = entry[2] // 4
                    self.ready[group] = max(self.ready.get(group, 0), tick)

    def tick(self):
        for _, _, item, kind, link in self.steps.get(self.next_tick, []):
            if kind == "send" and link == "y":
                if item % 4 == 0:
                    for load in self.loads[item // 4]:
                        load.wait()
                self.y_copy(item).start()
            elif kind == "send":
                self.plane_copy(item, link).start()
            elif kind == "arrive" and link == "y":
                self.y_arrival(item).wait_recv()
            elif kind == "arrive":
                self.plane_arrival(item, link).wait_recv()
            elif kind == "share":
                self.core_copy(item, link).start()
            elif kind == "shared":
                self.core_arrival(item, link).wait_recv()
            elif link == "y":
                self.y_copy(item).wait_send()
                self.core_copy(item, link).wait_send()
            else:
                self.plane_copy(item, link).wait_send()
                self.core_copy(item, link).wait_send()
        self.next_tick += 1

    def until(self, group):
        while self.next_tick <= self.ready[group]:
            self.tick()

    def finish(self):
        while self.next_tick <= self.last_tick:
            self.tick()


def piece_rows(ref, lead, rows, columns):
    height = rows // 24

    def full(piece, rank):
        start = pl.multiple_of(piece * height, 16)
        left = pl.multiple_of(rank * columns, 128)
        return ref.at[(*lead, pl.ds(start, height), pl.ds(left, columns))]

    return full


def column_groups(ref, lead, rows, columns, parts):
    height, width = rows // 24, columns // parts

    def group(part):
        def full(piece, rank):
            start = pl.multiple_of(piece * height, 16)
            left = pl.multiple_of(rank * columns + part * width, 128)
            return ref.at[(*lead, pl.ds(start, height), pl.ds(left, width))]

        return full

    return [group(part) for part in range(parts)]


def row_groups(ref, lead, rows, parts):
    height = rows // parts // 24

    def group(part):
        def full(piece, rank):
            start = rank * rows + part * (rows // parts) + piece * height
            return ref.at[(*lead, pl.ds(pl.multiple_of(start, 16), height), slice(None))]

        return full

    return [group(part) for part in range(parts)]


def tile_group(ref, rows, columns):
    height, width = rows // 8, columns // 3

    def full(piece, rank):
        start = pl.multiple_of(rank * rows + (piece % 8) * height, 16)
        left = pl.multiple_of((piece // 8) * width, 128)
        return ref.at[pl.ds(start, height), pl.ds(left, width)]

    return full


def gather_kernel(
    wq, wk, wv, wo, wu, wd, mat_a, mat_b,
    dq, bq, dv, bv,
    qkv, out, up, down, full_a, full_b, full_dq, full_bq, full_dv, full_bv,
    load_sem, small_send, small_recv, *sems, stored=(),
):
    levels, model, feat = wq.shape
    hidden, rank_part = wu.shape[2], mat_a.shape[1]
    rank = lax.axis_index("rank")
    parts = 2
    groups, loads = [], []
    used = [0]

    def load(src, dst):
        copy = pltpu.make_async_copy(src, dst, load_sem.at[used[0]])
        used[0] += 1
        copy.start()
        return copy

    def columns_of(size):
        return pl.ds(pl.multiple_of(rank * size, 128), size)

    def rows_of(size):
        return pl.ds(pl.multiple_of(rank * size, 16), size)

    groups.append(piece_rows(full_a, (), model, rank_part))
    loads.append([load(mat_a, full_a.at[:, columns_of(rank_part)])])
    groups.append(tile_group(full_b, rank_part, model))
    loads.append([load(mat_b, full_b.at[rows_of(rank_part), :])])
    for level in range(levels):
        groups.append(piece_rows(qkv, (level, slice(None)), model, feat))
        loads.append([
            load(w.at[level], qkv.at[level, i, :, columns_of(feat)])
            for i, w in enumerate((wq, wk, wv))
        ])
        groups += row_groups(out, (level,), feat, 1)
        loads.append([load(wo.at[level], out.at[level, rows_of(feat), :])])
        groups += column_groups(up, (level,), model, hidden, parts)
        loads.append([load(wu.at[level], up.at[level, :, columns_of(hidden)])])
        loads += [[]] * (parts - 1)
        groups += row_groups(down, (level,), hidden, parts)
        loads.append([load(wd.at[level], down.at[level, rows_of(hidden), :])])
        loads += [[]] * (parts - 1)
    vectors = [(dq, full_dq), (bq, full_bq), (dv, full_dv), (bv, full_bv)]
    small_loads = [load(src, dst.at[:, columns_of(src.shape[1])]) for src, dst in vectors]

    exchange = Exchange(groups, loads, sems)
    exchange.barrier()
    small = []
    for i, (src, dst) in enumerate(vectors):
        ref = dst.at[:, columns_of(src.shape[1])]
        small.append(exchange.copy(src, ref, small_send.at[i], small_recv.at[i], "y"))
        small[-1].start()
    stores = []
    for group, src, dst, sem in stored:
        exchange.until(group)
        stores.append(pltpu.make_async_copy(src, dst, sem))
        stores[-1].start()
    exchange.finish()
    for copy in small:
        copy.wait()
    for copy in stores:
        copy.wait()
    for copy in small_loads:
        copy.wait()


def gather_weights(wq, wk, wv, wo, wu, wd, mat_a, mat_b, dq, bq, dv, bv):
    levels, model, feat = wq.shape
    hidden, rank_part = wu.shape[2], mat_a.shape[1]
    ranks = 2
    low, f32 = jnp.bfloat16, jnp.float32
    shape = jax.ShapeDtypeStruct
    count = 4 * (2 + 6 * levels)
    any_spec = pl.BlockSpec(memory_space=pl.ANY)
    outs = (
        shape((levels, 3, model, ranks * feat), low),
        shape((levels, ranks * feat, model), low),
        shape((levels, model, ranks * hidden), low),
        shape((levels, ranks * hidden, model), low),
        shape((model, ranks * rank_part), low),
        shape((ranks * rank_part, model), low),
        shape((levels, ranks * rank_part), f32),
        shape((levels, ranks * feat), f32),
        shape((levels, ranks * rank_part), f32),
        shape((levels, ranks * feat), f32),
    )
    dma = lambda n: pltpu.SemaphoreType.DMA((n,))
    def kernel(*refs):
        ins, refs = refs[:12], refs[12:]
        outs_hbm, refs = refs[:6], refs[6:]
        vectors, refs = refs[:4], refs[4:]
        vmem, store_sem, refs = refs[:6], refs[6], refs[7:]
        stored = [(0, vmem[4], outs_hbm[4], store_sem.at[0]), (1, vmem[5], outs_hbm[5], store_sem.at[1])]
        for level in range(levels):
            for i, last in enumerate((0, 1, 3, 5)):
                stored.append((2 + 6 * level + last, vmem[i].at[level], outs_hbm[i].at[level],
                               store_sem.at[2 + 4 * level + i]))
        gather_kernel(*ins, *vmem, *vectors, *refs, stored=stored)

    vmem_spec = pl.BlockSpec(memory_space=pltpu.VMEM)
    return pl.pallas_call(
        kernel,
        out_shape=outs,
        in_specs=[any_spec] * 12,
        out_specs=(any_spec,) * 6 + (vmem_spec,) * 4,
        scratch_shapes=[pltpu.VMEM(o.shape, o.dtype) for o in outs[:6]]
        + [dma(2 + 4 * levels), dma(2 + 6 * levels + 4), dma(4), dma(4)]
        + [dma(count) for _ in range(6)]
        + [dma(3 * count)] * 2,
        compiler_params=pltpu.CompilerParams(
            collective_id=0, has_side_effects=True, vmem_limit_bytes=50 * 2**20),
        name="gather_weights",
    )(wq, wk, wv, wo, wu, wd, mat_a, mat_b, dq, bq, dv, bv)


def normalize(values):
    center = values - jnp.mean(values, axis=-1, keepdims=True)
    spread = jnp.mean(center * center, axis=-1, keepdims=True)
    return center * lax.rsqrt(spread + epsilon)


def gelu_exact(values):
    return jax.nn.gelu(values, approximate=False)


def matmul(operand, matrix):
    return jnp.dot(operand, matrix, preferred_element_type=jnp.float32)


def matmul_back(operand, matrix):
    return jnp.einsum("td,ed->te", operand, matrix, preferred_element_type=jnp.float32)


def to_heads(rows, pair_count):
    return rows.reshape(pair_count, -1, rows.shape[1] // HEAD_DIM, HEAD_DIM)


def pair_scores(query_rows, key_rows, key_mask):
    scores = jnp.einsum(
        "qhe,khe->hqk", query_rows, key_rows, preferred_element_type=jnp.float32
    ) * HEAD_DIM ** (-0.5)
    return jnp.where(key_mask[None, None, :], scores, masked)


def attend_pair(pieces):
    query_rows, key_rows, value_rows, key_mask = pieces
    scores = pair_scores(query_rows, key_rows, key_mask)
    row_peak = jnp.max(scores, axis=-1, keepdims=True)
    exponent = jnp.exp(scores - row_peak)
    row_total = jnp.sum(exponent, axis=-1, keepdims=True)
    weights_low = (exponent / row_total).astype(jnp.bfloat16)
    mixed_rows = jnp.einsum(
        "hqk,khe->qhe", weights_low, value_rows, preferred_element_type=jnp.float32
    )
    return (mixed_rows.astype(jnp.bfloat16), row_peak[..., 0] + jnp.log(row_total[..., 0]))


def attend_back(pieces):
    query_rows, key_rows, value_rows, key_mask, log_total, incoming = pieces
    scores = pair_scores(query_rows, key_rows, key_mask)
    probs_full = jnp.exp(scores - log_total[..., None])
    dprob = jnp.einsum("qhe,khe->hqk", incoming, value_rows, preferred_element_type=jnp.float32)
    grad_value = jnp.einsum(
        "hqk,qhe->khe",
        probs_full.astype(jnp.bfloat16),
        incoming,
        preferred_element_type=jnp.float32,
    )
    row_delta = jnp.sum(probs_full * dprob, axis=-1, keepdims=True)
    dscore = (probs_full * (dprob - row_delta)).astype(jnp.bfloat16)
    grad_query = jnp.einsum(
        "hqk,khe->qhe", dscore, key_rows, preferred_element_type=jnp.float32
    ) * HEAD_DIM ** (-0.5)
    grad_key = jnp.einsum(
        "hqk,qhe->khe", dscore, query_rows, preferred_element_type=jnp.float32
    ) * HEAD_DIM ** (-0.5)
    return (
        grad_query.astype(jnp.bfloat16),
        grad_key.astype(jnp.bfloat16),
        grad_value.astype(jnp.bfloat16),
    )


def layer_forward(inputs, key_mask, weights, shared_a, shared_b):
    w_qkv, w_out, w_up, w_down, scale_dq, scale_bq, scale_dv, scale_bv = weights
    rows_low = inputs.astype(jnp.bfloat16)
    inner = matmul(rows_low, shared_a)
    lift_query = matmul((inner * scale_dq).astype(jnp.bfloat16), shared_b)
    lift_value = matmul((inner * scale_dv).astype(jnp.bfloat16), shared_b)
    query_rows = (matmul(rows_low, w_qkv[0]) + lift_query * scale_bq).astype(jnp.bfloat16)
    key_rows = matmul(rows_low, w_qkv[1]).astype(jnp.bfloat16)
    value_rows = (matmul(rows_low, w_qkv[2]) + lift_value * scale_bv).astype(jnp.bfloat16)
    heads = lambda rows: to_heads(rows, 1)[0]
    mixed_rows, log_total = attend_pair(
        (heads(query_rows), heads(key_rows), heads(value_rows), key_mask)
    )
    attended = mixed_rows.reshape(inputs.shape[0], -1)
    first_sum = inputs + matmul(attended, w_out)
    normed = normalize(first_sum)
    before = matmul(normed.astype(jnp.bfloat16), w_up)
    hidden = gelu_exact(before).astype(jnp.bfloat16)
    second_sum = normed + matmul(hidden, w_down)
    saved = (inner, lift_query, lift_value, query_rows, key_rows, value_rows, log_total,
             first_sum, before, second_sum)
    return (normalize(second_sum), saved)


def layer_backward(saved, key_mask, weights, shared_a, shared_b, upstream):
    w_qkv, w_out, w_up, w_down, scale_dq, scale_bq, scale_dv, scale_bv = weights
    (inner, lift_query, lift_value, query_rows, key_rows, value_rows, log_total,
     first_sum, before, second_sum) = saved
    unused, second_back = jax.vjp(normalize, second_sum)
    grad_second = second_back(upstream)[0]
    grad_hidden = matmul_back(grad_second.astype(jnp.bfloat16), w_down)
    unused, gelu_back = jax.vjp(gelu_exact, before)
    grad_before = gelu_back(grad_hidden)[0].astype(jnp.bfloat16)
    unused, first_back = jax.vjp(normalize, first_sum)
    grad_first = first_back(grad_second + matmul_back(grad_before, w_up))[0]
    grad_attended = matmul_back(grad_first.astype(jnp.bfloat16), w_out).astype(jnp.bfloat16)
    heads = lambda rows: to_heads(rows, 1)[0]
    grad_query, grad_key, grad_value = attend_back(
        (heads(query_rows), heads(key_rows), heads(value_rows), key_mask, log_total,
         heads(grad_attended))
    )
    row_count = upstream.shape[0]
    grad_query = grad_query.reshape(row_count, -1)
    grad_key = grad_key.reshape(row_count, -1)
    grad_value = grad_value.reshape(row_count, -1)
    grad_bq = jnp.sum(grad_query.astype(jnp.float32) * lift_query, axis=0)
    grad_bv = jnp.sum(grad_value.astype(jnp.float32) * lift_value, axis=0)
    pass_query = (grad_query * scale_bq).astype(jnp.bfloat16)
    pass_value = (grad_value * scale_bv).astype(jnp.bfloat16)
    rank_query = matmul_back(pass_query, shared_b)
    rank_value = matmul_back(pass_value, shared_b)
    grad_dq = jnp.sum(rank_query * inner, axis=0)
    grad_dv = jnp.sum(rank_value * inner, axis=0)
    grad_inner = (rank_query * scale_dq + rank_value * scale_dv).astype(jnp.bfloat16)
    input_sum = (
        matmul_back(grad_query, w_qkv[0])
        + matmul_back(grad_key, w_qkv[1])
        + matmul_back(grad_value, w_qkv[2])
        + matmul_back(grad_inner, shared_a)
    )
    return (grad_first + input_sum, (grad_dq, grad_bq, grad_dv, grad_bv))


def swap_rows(rows):
    other = lax.ppermute(rows.astype(jnp.bfloat16), "rank", [(0, 1), (1, 0)]).astype(rows.dtype)
    mine_first = lax.axis_index("rank") == 0
    return jnp.concatenate(
        [jnp.where(mine_first, rows, other), jnp.where(mine_first, other, rows)], axis=0
    )


def on_device(tokens, valid_len, w_query, w_key, w_value, w_out, w_up, w_down, mat_a, mat_b,
              scale_dq, scale_bq, scale_dv, scale_bv, cotangent):
    rank = lax.axis_index("rank")
    pair_count = valid_len.shape[0]
    seq_len = tokens.shape[0] // pair_count
    level_count = w_query.shape[0]
    qkv, out, up, down, full_a, full_b, *vectors = gather_weights(
        w_query, w_key, w_value, w_out, w_up, w_down, mat_a, mat_b,
        scale_dq, scale_bq, scale_dv, scale_bv)
    mine = lambda rows: lax.dynamic_slice_in_dim(rows, rank * seq_len, seq_len, 0)
    length = lax.dynamic_index_in_dim(valid_len, rank, 0, keepdims=False)
    key_mask = jnp.arange(seq_len, dtype=jnp.int32) < length
    current = mine(tokens).astype(jnp.float32)
    saved, level_weights = [], []
    for level in range(level_count):
        weights = (qkv[level], out[level], up[level], down[level]) + tuple(v[level] for v in vectors)
        level_weights.append(weights)
        current, kept = layer_forward(current, key_mask, weights, full_a, full_b)
        saved.append(kept)
    upstream = mine(cotangent).astype(jnp.float32)
    collected = [None] * level_count
    for level in reversed(range(level_count)):
        upstream, collected[level] = layer_backward(
            saved[level], key_mask, level_weights[level], full_a, full_b, upstream)
    totals = tuple(jnp.stack([grads[member] for grads in collected]) for member in range(4))
    totals = lax.psum(totals, ("batch", "rank"))
    own = lambda vector: lax.dynamic_slice_in_dim(
        vector, rank * (vector.shape[1] // 2), vector.shape[1] // 2, 1)
    return (swap_rows(current), swap_rows(upstream)) + tuple(own(vector) for vector in totals)


def solution(mesh):
    split = P(None, None, "rank")
    down_split = P(None, "rank", None)
    vector = P(None, "rank")
    return jax.shard_map(
        on_device,
        mesh=mesh,
        in_specs=(P("batch", None), P("batch"), split, split, split, down_split, split, down_split,
                  P(None, "rank"), P("rank", None), vector, vector, vector, vector, P("batch", None)),
        out_specs=(P("batch", None), P("batch", None), vector, vector, vector, vector),
        check_vma=False,
    )
```

```python
import functools
import math

import jax
import jax.numpy as jnp
from jax import lax
from jax.experimental import pallas as pl
from jax.experimental.pallas import tpu as pltpu
from jax.sharding import PartitionSpec as P

HEAD_DIM = 64
MESH = pl.DeviceIdType.MESH

epsilon = 1e-05
masked = -1e30

low, f32 = jnp.bfloat16, jnp.float32


def flip(index, bit):
    step = 1 << bit
    return index + step - 2 * step * ((index // step) % 2)


class Exchange:
    LAG = 4
    HOP = 2

    def __init__(self, groups, loads, sems):
        self.groups, self.loads = groups, loads
        self.y_send, self.y_recv, self.x_send, self.x_recv, self.z_send, self.z_recv, self.c_send, self.c_recv = sems
        self.batch = lax.axis_index("batch")
        self.rank = lax.axis_index("rank")
        b = self.batch
        self.core = b % 2
        bit_x, bit_z = (b // 2) % 2, (b // 4) % 2
        self.partner = {
            "y": (b, 1 - self.rank),
            "x": (flip(b, 1), self.rank),
            "z": (flip(b, 2), self.rank),
            "c": (flip(b, 0), self.rank),
        }
        chip = lambda cx, cz: cx + 2 * cz
        own, across, along, far = (
            chip(bit_x, bit_z),
            chip(1 - bit_x, bit_z),
            chip(bit_x, 1 - bit_z),
            chip(1 - bit_x, 1 - bit_z),
        )
        parity = (bit_x + bit_z) % 2
        first = lambda who: 2 * who
        second = lambda who: 2 * who + 1
        pair = lambda par, which: 8 + 2 * par + which
        self.y_units = [first(own), second(own), pair(parity, 0), pair(parity, 1)]
        self.x_units = [first(across), second(across), pair(1 - parity, 0), second(far)]
        self.z_units = [first(along), second(along), first(far), pair(1 - parity, 1)]
        self.x_out = [first(own), second(own), pair(parity, 0), second(along)]
        self.z_out = [first(own), second(own), first(across), pair(parity, 1)]
        self.count = 4 * len(groups)
        self.pending = []
        self.next_tick = 0
        self.plan()

    def barrier(self):
        bar = pltpu.get_barrier_semaphore()
        for who in self.partner.values():
            pl.semaphore_signal(bar, inc=1, device_id=who, device_id_type=MESH)
        pl.semaphore_wait(bar, len(self.partner))

    def copy(self, src, dst, send, recv, link):
        return pltpu.make_async_remote_copy(
            src_ref=src, dst_ref=dst, send_sem=send, recv_sem=recv,
            device_id=self.partner[link], device_id_type=MESH,
        )

    def full(self, group, unit, core, rank):
        return self.groups[group](2 * unit + core, rank)

    def y_copy(self, item):
        g, j = divmod(item, 4)
        ref = self.full(g, self.y_units[j], self.core, self.rank)
        return self.copy(ref, ref, self.y_send.at[item], self.y_recv.at[item], "y")

    def plane_copy(self, item, link):
        g, j = divmod(item, 4)
        unit = (self.x_out if link == "x" else self.z_out)[j]
        send, recv = (self.x_send, self.x_recv) if link == "x" else (self.z_send, self.z_recv)
        ref = self.full(g, unit, self.core, 1 - self.rank)
        return self.copy(ref, ref, send.at[item], recv.at[item], link)

    def core_copy(self, item, link):
        g, j = divmod(item, 4)
        unit = {"y": self.y_units, "x": self.x_units, "z": self.z_units}[link][j]
        slot = 3 * item + {"y": 0, "x": 1, "z": 2}[link]
        ref = self.full(g, unit, self.core, 1 - self.rank)
        return self.copy(ref, ref, self.c_send.at[slot], self.c_recv.at[slot], "c")

    def core_arrival(self, item, link):
        g, j = divmod(item, 4)
        unit = {"y": self.y_units, "x": self.x_units, "z": self.z_units}[link][j]
        slot = 3 * item + {"y": 0, "x": 1, "z": 2}[link]
        ref = self.full(g, unit, 1 - self.core, 1 - self.rank)
        return self.copy(ref, ref, self.c_send.at[slot], self.c_recv.at[slot], "c")

    def y_arrival(self, item):
        g, j = divmod(item, 4)
        ref = self.full(g, self.y_units[j], self.core, 1 - self.rank)
        return self.copy(ref, ref, self.y_send.at[item], self.y_recv.at[item], "y")

    def plane_arrival(self, item, link):
        g, j = divmod(item, 4)
        unit = (self.x_units if link == "x" else self.z_units)[j]
        send, recv = (self.x_send, self.x_recv) if link == "x" else (self.z_send, self.z_recv)
        ref = self.full(g, unit, self.core, 1 - self.rank)
        return self.copy(ref, ref, send.at[item], recv.at[item], link)

    def plan(self):
        lag, hop = self.LAG, self.HOP
        begin = {}
        for item in range(self.count):
            begin["y", item] = item
        for group in range(self.count // 4):
            at = lambda link, j: begin[link, 4 * group + j] + lag
            for link, j in (("x", 0), ("x", 1), ("x", 2), ("z", 0), ("z", 1), ("z", 3)):
                begin[link, 4 * group + j] = at("y", j)
            begin["z", 4 * group + 2] = at("x", 0)
            begin["x", 4 * group + 3] = at("z", 1)
        steps = {}
        order = {"y": 0, "x": 1, "z": 2}
        for (link, item), tick in begin.items():
            arrived = tick + lag
            steps.setdefault(tick, []).append((1, order[link], item, "send", link))
            steps.setdefault(arrived, []).append((0, order[link], item, "arrive", link))
            steps.setdefault(arrived, []).append((2, order[link], item, "share", link))
            steps.setdefault(arrived + hop, []).append((3, order[link], item, "shared", link))
            steps.setdefault(arrived + lag, []).append((4, order[link], item, "sent", link))
        self.steps = {tick: sorted(found) for tick, found in steps.items()}
        self.last_tick = max(steps)
        self.ready = {}
        for tick, found in steps.items():
            for entry in found:
                if entry[3] == "shared":
                    group = entry[2] // 4
                    self.ready[group] = max(self.ready.get(group, 0), tick)

    def tick(self):
        for _, _, item, kind, link in self.steps.get(self.next_tick, []):
            if kind == "send" and link == "y":
                if item % 4 == 0:
                    for load in self.loads[item // 4]:
                        load.wait()
                self.y_copy(item).start()
            elif kind == "send":
                self.plane_copy(item, link).start()
            elif kind == "arrive" and link == "y":
                self.y_arrival(item).wait_recv()
            elif kind == "arrive":
                self.plane_arrival(item, link).wait_recv()
            elif kind == "share":
                self.core_copy(item, link).start()
            elif kind == "shared":
                self.core_arrival(item, link).wait_recv()
            elif link == "y":
                self.y_copy(item).wait_send()
                self.core_copy(item, link).wait_send()
            else:
                self.plane_copy(item, link).wait_send()
                self.core_copy(item, link).wait_send()
        self.next_tick += 1

    def until(self, group):
        while self.next_tick <= self.ready[group]:
            self.tick()

    def finish(self):
        while self.next_tick <= self.last_tick:
            self.tick()


def piece_rows(ref, lead, rows, columns):
    height = rows // 24

    def full(piece, rank):
        start = pl.multiple_of(piece * height, 16)
        left = pl.multiple_of(rank * columns, 128)
        return ref.at[(*lead, pl.ds(start, height), pl.ds(left, columns))]

    return full


def column_groups(ref, lead, rows, columns, parts):
    height, width = rows // 24, columns // parts

    def group(part):
        def full(piece, rank):
            start = pl.multiple_of(piece * height, 16)
            left = pl.multiple_of(rank * columns + part * width, 128)
            return ref.at[(*lead, pl.ds(start, height), pl.ds(left, width))]

        return full

    return [group(part) for part in range(parts)]


def row_groups(ref, lead, rows, parts):
    height = rows // parts // 24

    def group(part):
        def full(piece, rank):
            start = rank * rows + part * (rows // parts) + piece * height
            return ref.at[(*lead, pl.ds(pl.multiple_of(start, 16), height), slice(None))]

        return full

    return [group(part) for part in range(parts)]


def tile_group(ref, rows, columns):
    height, width = rows // 8, columns // 3

    def full(piece, rank):
        start = pl.multiple_of(rank * rows + (piece % 8) * height, 16)
        left = pl.multiple_of((piece // 8) * width, 128)
        return ref.at[pl.ds(start, height), pl.ds(left, width)]

    return full


def dot(left, right):
    return jnp.dot(left, right, preferred_element_type=f32)


def dot_back(left, right):
    return lax.dot_general(left, right, (((1,), (1,)), ((), ())), preferred_element_type=f32)


def row_blocks(rows, height, body):
    def step(index, carry):
        body(pl.ds(pl.multiple_of(index * height, height), height))
        return carry

    lax.fori_loop(0, rows // height, step, 0)


def normalize(values):
    center = values - jnp.mean(values, axis=-1, keepdims=True)
    spread = jnp.mean(center * center, axis=-1, keepdims=True)
    scale = lax.rsqrt(spread + epsilon)
    return center * scale, scale


def normalize_back(grad, normed, scale):
    shared = jnp.mean(grad * normed, axis=-1, keepdims=True)
    return (grad - jnp.mean(grad, axis=-1, keepdims=True) - normed * shared) * scale


def gelu_and_slope(values):
    bell = jnp.exp(-0.5 * values * values)
    t = 1.0 / (1.0 + (0.3275911 * 0.5**0.5) * jnp.abs(values))
    poly = t * (0.254829592 + t * (-0.284496736 + t * (1.421413741 + t * (-1.453152027 + t * 1.061405429))))
    tail = 0.5 * poly * bell
    cdf = jnp.where(values >= 0, 1.0 - tail, tail)
    return values * cdf, cdf + values * bell * (2.0 * math.pi) ** -0.5


def lane_half(shape, which):
    lanes = lax.broadcasted_iota(jnp.int32, shape, 1)
    return (lanes < HEAD_DIM) if which == 0 else (lanes >= HEAD_DIM)


class Layers:
    def __init__(self, refs):
        self.__dict__.update(refs)
        self.rows, self.model = self.x.shape
        self.heads = self.model // HEAD_DIM

    def adapt(self, level, tick, need):
        ranks = self.full_a.shape[1]
        dq, dv = self.dq[level], self.dv[level]
        bq, bv = self.bq[level], self.bv[level]
        half = self.rows // 2
        parts = [pl.ds(i * half, half) for i in range(2)]
        need("a")
        for part in parts:
            inner = dot(self.xl[part, :], self.full_a[...])
            self.inner[part, :] = inner.astype(low)
            self.hid[part, :ranks] = (inner * dq).astype(low)
            self.hid[part, ranks : 2 * ranks] = (inner * dv).astype(low)
            tick()
        need("b")
        for part in parts:
            self.lift[0, part, :] = dot(self.hid[part, :ranks], self.full_b[...]).astype(low)
            self.lift[1, part, :] = dot(self.hid[part, ranks : 2 * ranks], self.full_b[...]).astype(low)
            tick()
        need("qkv")
        for part in parts:
            rows = self.xl[part, :]
            query = dot(rows, self.qkv[level, 0]) + self.lift[0, part, :].astype(f32) * bq
            self.att[0, part, :] = (query.astype(low).astype(f32) * HEAD_DIM**-0.5).astype(low)
            self.att[1, part, :] = dot(rows, self.qkv[level, 1]).astype(low)
            tick()
            value = dot(rows, self.qkv[level, 2]) + self.lift[2 - 1, part, :].astype(f32) * bv
            self.att[2, part, :] = value.astype(low)
            tick()

    def attend(self, tick):
        width = 2 * HEAD_DIM
        block = self.rows // 2
        bias = self.bias[...]
        bias = jnp.concatenate([bias] * (block // bias.shape[1]), axis=1)
        for pair in range(self.heads // 2):
            slab = slice(pair * width, (pair + 1) * width)
            keys = self.att[1, :, slab]
            values_t = jnp.transpose(self.att[2, :, slab].astype(f32)).astype(low)
            for part in range(2):
                rows = pl.ds(part * block, block)
                query = self.att[0, rows, slab]
                mixed = []
                for which in range(2):
                    chosen = jnp.where(lane_half(query.shape, which), query, jnp.zeros_like(query))
                    scores = dot_back(keys, chosen) + bias
                    peak = jnp.max(scores, axis=0, keepdims=True)
                    exponent = jnp.exp(scores - peak)
                    total = jnp.sum(exponent, axis=0, keepdims=True)
                    probs = (exponent * (1.0 / total)).astype(low)
                    self.probs[2 * pair + which, :, rows] = probs
                    mixed.append(dot(values_t[which * HEAD_DIM : (which + 1) * HEAD_DIM, :], probs))
                self.mix[rows, slab] = jnp.transpose(jnp.concatenate(mixed, axis=0)).astype(low)
            tick()

    def project(self, level, tick, need):
        need("out")

        def body(part):
            first = self.x[part, :] + dot(self.mix[part, :], self.out[level])
            normed, scale = normalize(first)
            self.f2[part, :] = normed
            self.normed[2 * level, part, :] = normed.astype(low)
            self.scale[2 * level, part, :] = scale

        row_blocks(self.rows, self.rows // 4, body)
        tick()

    def feed(self, level, rank, tick, need):
        hidden = self.hid.shape[1]
        width = hidden // 6
        for chunk in range(6):
            if chunk == 3:
                need("up0")
            if chunk == 4:
                need("up1")
            left = (rank * 3 + chunk) % 6 * width
            columns = pl.ds(pl.multiple_of(left, 128), width)

            def body(part):
                before = dot(self.normed[2 * level, part, :], self.up[level, :, columns])
                active, slope = gelu_and_slope(before)
                self.hid[part, columns] = active.astype(low)
                self.slope[part, columns] = slope.astype(low)

            row_blocks(self.rows, self.rows // 4, body)
            tick()
        half = hidden // 2
        pieces = [(0, half, None), (half, half // 2, "down0"), (half + half // 2, half // 2, "down1")]
        for start, depth, group in pieces:
            if group:
                need(group)
            left = (rank * half + start) % hidden
            units = pl.ds(pl.multiple_of(left, 128), depth)

            def body(part):
                self.f2[part, :] += dot(self.hid[part, units], self.down[level, units, :])

            row_blocks(self.rows, self.rows // 2, body)
            tick()

        def body(part):
            normed, scale = normalize(self.f2[part, :])
            self.x[part, :] = normed
            self.xl[part, :] = normed.astype(low)
            self.normed[2 * level + 1, part, :] = normed.astype(low)
            self.scale[2 * level + 1, part, :] = scale

        row_blocks(self.rows, self.rows // 4, body)


    def feed_back(self, level):
        def norm_body(part):
            grad = normalize_back(
                self.x[part, :], self.normed[2 * level + 1, part, :].astype(f32), self.scale[2 * level + 1, part, :])
            self.f2[part, :] = grad
            self.xl[part, :] = grad.astype(low)

        row_blocks(self.rows, self.rows // 4, norm_body)
        hidden = self.hid.shape[1]
        width = hidden // 6

        def chunk_body(chunk, carry):
            columns = pl.ds(pl.multiple_of(chunk * width, width), width)
            grad = dot_back(self.xl[...], self.down[level, columns, :])
            self.hid[:, columns] = (grad * self.slope[:, columns].astype(f32)).astype(low)
            return carry

        lax.fori_loop(0, 6, chunk_body, 0)

        def up_body(part):
            grad = self.f2[part, :] + dot_back(self.hid[part, :], self.up[level])
            grad = normalize_back(
                grad, self.normed[2 * level, part, :].astype(f32), self.scale[2 * level, part, :])
            self.f2[part, :] = grad
            self.mix[part, :] = dot_back(grad.astype(low), self.out[level]).astype(low)

        row_blocks(self.rows, self.rows // 2, up_body)

    def attend_back(self):
        width = 2 * HEAD_DIM

        def pair_body(pair, carry):
            slab = pl.ds(pl.multiple_of(pair * width, width), width)
            query, keys, values = (self.att[i, :, slab] for i in range(3))
            grad = self.mix[:, slab]
            keys_t = jnp.transpose(keys.astype(f32)).astype(low)
            grad_values, grad_keys, grad_query = [], [], []
            for which in range(2):
                probs = self.probs[2 * pair + which]
                chosen = jnp.where(lane_half(values.shape, which), values, jnp.zeros_like(values))
                dprob = dot_back(chosen, grad)
                wide = probs.astype(f32)
                delta = jnp.sum(wide * dprob, axis=0, keepdims=True)
                dscore = (wide * (dprob - delta)).astype(low)
                grad_values.append(dot(probs, grad))
                grad_keys.append(dot(dscore, query))
                grad_query.append(dot(keys_t[which * HEAD_DIM : (which + 1) * HEAD_DIM, :], dscore))
            first = lane_half(values.shape, 0)
            query_grad = jnp.transpose(jnp.concatenate(grad_query, axis=0)) * HEAD_DIM**-0.5
            self.att[0, :, slab] = query_grad.astype(low)
            self.att[1, :, slab] = jnp.where(first, *grad_keys).astype(low)
            self.att[2, :, slab] = jnp.where(first, *grad_values).astype(low)
            return carry

        lax.fori_loop(0, self.heads // 2, pair_body, 0)

    def adapt_back(self, level, sums, part):
        ranks = self.full_a.shape[1]
        dq, dv = self.dq[level], self.dv[level]
        bq, bv = self.bq[level], self.bv[level]
        query, values = (self.att[i, part, :].astype(f32) for i in (0, 2))
        total = lambda grid: jnp.sum(grid, axis=0, keepdims=True)
        sums[1] += total(query * self.lift[0, part, :].astype(f32))
        sums[3] += total(values * self.lift[1, part, :].astype(f32))
        inner = self.inner[part, :].astype(f32)
        rank_query = dot_back((query * bq).astype(low), self.full_b[...])
        sums[0] += total(rank_query * inner)
        rank_value = dot_back((values * bv).astype(low), self.full_b[...])
        sums[2] += total(rank_value * inner)
        grad_inner = (rank_query * dq + rank_value * dv).astype(low)
        grad = self.f2[part, :] + dot_back(grad_inner, self.full_a[...])
        for i in range(3):
            grad += dot_back(self.att[i, part, :], self.qkv[level, i])
        self.x[part, :] = grad


def layers_kernel(levels, names, groups_of, *refs):
    refs = dict(zip(names, refs))
    get = refs.pop
    ins = [get(n) for n in INPUTS]
    (tokens, lengths, wq, wk, wv, wo, wu, wd, mat_a, mat_b, dq, bq, dv, bv, cotangent) = ins
    rank, batch = lax.axis_index("rank"), lax.axis_index("batch")
    both = refs["x"].shape[0]
    seq = both
    model, feat = wq.shape[1:]
    hidden, rank_part = wu.shape[2], mat_a.shape[1]
    out_x, out_g = get("out_x"), get("out_g")
    out_vectors = [get(n) for n in ("out_dq", "out_bq", "out_dv", "out_bv")]
    spills = [get("spill_probs"), get("spill_att"), get("spill_lift"), get("spill_inner"), get("spill_slope")]
    load_sem, spill_sem, small_send, small_recv = (get(n) for n in ("load_sem", "spill_sem", "small_send", "small_recv"))
    sems = [get(f"sem{i}") for i in range(8)]
    swap_send, swap_recv, sum_send, sum_recv = (get(n) for n in ("swap_send", "swap_recv", "sum_send", "sum_recv"))
    store_sem = get("store_sem")
    gone, came = get("gone"), get("came")
    sum_buf, sum_in = get("sum_buf"), get("sum_in")
    layers = Layers(refs)
    L = layers

    used = [0]

    def load(src, dst):
        copy = pltpu.make_async_copy(src, dst, load_sem.at[used[0]])
        used[0] += 1
        copy.start()
        return copy

    def columns_of(size):
        return pl.ds(pl.multiple_of(rank * size, 128), size)

    def rows_of(size):
        return pl.ds(pl.multiple_of(rank * size, 16), size)

    own_rows = rows_of(seq)
    other_rows = pl.ds(pl.multiple_of((1 - rank) * seq, 16), seq)

    groups, loads, names_of = [], [], {}

    def add(name, found, copies):
        for i, group in enumerate(found):
            names_of[name + (str(i) if len(found) > 1 else "")] = len(groups)
            groups.append(group)
            loads.append(copies if i == 0 else [])

    add("a", [piece_rows(L.full_a, (), model, rank_part)], [load(mat_a, L.full_a.at[:, columns_of(rank_part)])])
    load_x = load(tokens.at[own_rows, :], L.xl)
    add("b", [tile_group(L.full_b, rank_part, model)], [load(mat_b, L.full_b.at[rows_of(rank_part), :])])
    for level in range(levels):
        tag = lambda name: f"{name}/{level}"
        add(f"qkv/{level}", [piece_rows(L.qkv, (level, slice(None)), model, feat)], [
            load(w.at[level], L.qkv.at[level, i, :, columns_of(feat)]) for i, w in enumerate((wq, wk, wv))])
        add(f"out/{level}", row_groups(L.out, (level,), feat, 1), [
            load(wo.at[level], L.out.at[level, rows_of(feat), :])])
        add(f"up/{level}/", column_groups(L.up, (level,), model, hidden, 2), [
            load(wu.at[level], L.up.at[level, :, columns_of(hidden)])])
        add(f"down/{level}/", row_groups(L.down, (level,), hidden, 2), [
            load(wd.at[level], L.down.at[level, rows_of(hidden), :])])
    vectors = [(dq, L.dq), (bq, L.bq), (dv, L.dv), (bv, L.bv)]

    exchange = Exchange(groups, loads, sems)
    bits = (lax.axis_size("batch") - 1).bit_length()
    for bit in range(3, bits):
        exchange.partner[bit] = (flip(batch, bit), rank)
    exchange.barrier()
    small = []
    for i, (src, dst) in enumerate(vectors):
        ref = dst.at[:, :, columns_of(src.shape[2])]
        small.append(exchange.copy(src, ref, small_send.at[i], small_recv.at[i], "y"))
        small[-1].start()
    small_loads = [load(src, dst.at[:, :, columns_of(src.shape[2])]) for src, dst in vectors]

    slots = lax.broadcasted_iota(jnp.int32, L.bias.shape, 0)
    length = lengths[rank]
    L.bias[...] = jnp.where(slots < length, 0.0, masked)

    for _ in range(3):
        exchange.tick()
    load_x.wait()

    def widen(part):
        L.x[part, :] = L.xl[part, :].astype(f32)

    row_blocks(seq, seq // 4, widen)
    for copy in small + small_loads:
        copy.wait()

    spill_src = [L.probs, L.att, L.lift, L.inner, L.slope]
    spill = [pltpu.make_async_copy(src, dst, spill_sem.at[i]) for i, (src, dst) in enumerate(zip(spill_src, spills))]
    fetch = [pltpu.make_async_copy(dst, src, spill_sem.at[i]) for i, (src, dst) in enumerate(zip(spill_src, spills))]
    PROBS, ATT, LIFT, INNER, SLOPE = range(5)

    for level in range(levels):
        def need(name):
            full = {"a": "a", "b": "b", "qkv": f"qkv/{level}", "out": f"out/{level}", "up0": f"up/{level}/0",
                    "up1": f"up/{level}/1", "down0": f"down/{level}/0", "down1": f"down/{level}/1"}[name]
            exchange.until(names_of[full])

        if level:
            for i in (ATT, LIFT, INNER, PROBS):
                spill[i].wait()
        L.adapt(level, exchange.tick, need)
        if not level:
            spill[LIFT].start()
            spill[INNER].start()
        L.attend(exchange.tick)
        if not level:
            spill[ATT].start()
            spill[PROBS].start()
        L.project(level, exchange.tick, need)
        if level:
            spill[SLOPE].wait()
        L.feed(level, rank, exchange.tick, need)
        if not level:
            spill[SLOPE].start()
    exchange.finish()

    def swap(index, part, part_rows):
        src = gone if index else L.normed.at[2 * levels - 1]
        return exchange.copy(src.at[part, :], came.at[index, part], swap_send.at[2 * index + part_rows],
                             swap_recv.at[2 * index + part_rows], "y")

    half = seq // 2
    halves = [pl.ds(i * half, half) for i in range(2)]
    store_own = [pltpu.make_async_copy(L.x, out_x.at[own_rows, :], store_sem.at[0])]
    store_own[0].start()
    swaps = [swap(0, part, i) for i, part in enumerate(halves)]
    for copy in swaps:
        copy.start()
    load_g = load(cotangent.at[own_rows, :], L.xl)
    load_g.wait()
    store_own[0].wait()
    row_blocks(seq, seq // 4, widen)

    def sum_copy(level, step):
        who = ["y", "c", "x", "z", *range(3, bits)][step]
        src = sum_buf.at[level, 1 - rank] if step == 0 else sum_buf.at[level, rank]
        return exchange.copy(src, sum_in.at[level, step], sum_send.at[level, step], sum_recv.at[level, step], who)

    def sum_step(level, step):
        if step:
            sum_copy(level, step - 1).wait()
            sum_buf[level, rank] += sum_in[level, step - 1]
        if step < 1 + bits:
            sum_copy(level, step).start()

    for level in reversed(range(levels)):
        last = level == 0
        L.feed_back(level)
        if not last:
            fetch[SLOPE].start()
        elif levels > 1:
            fetch[ATT].wait()
            fetch[PROBS].wait()
        L.attend_back()
        if not last:
            fetch[PROBS].start()
        else:
            fetch[LIFT].wait()
            fetch[INNER].wait()
        sums = [jnp.zeros((1, 2 * w), f32) for w in (rank_part, feat, rank_part, feat)]
        for i, part in enumerate(halves):
            L.adapt_back(level, sums, part)
            if last:
                gone[part, :] = L.x[part, :].astype(low)
                copy = swap(1, part, i)
                copy.start()
                swaps.append(copy)
        at = 0
        for width, total in zip((rank_part, feat, rank_part, feat), sums):
            for side in range(2):
                sum_buf[level, side, :, pl.ds(at, width)] = total[:, side * width : (side + 1) * width]
            at += width
        if not last:
            for i in (ATT, LIFT, INNER):
                fetch[i].start()
            fetch[SLOPE].wait()
        for step in range(2 + bits):
            sum_step(level, step)
    store_g = pltpu.make_async_copy(L.x, out_g.at[own_rows, :], store_sem.at[1])
    store_g.start()
    at = 0
    for width, dst in zip((rank_part, feat, rank_part, feat), out_vectors):
        for level in range(levels):
            dst[level] = sum_buf[level, rank, :, pl.ds(at, width)]
        at += width
    store_other = []
    for copy in swaps[:2]:
        copy.wait()

    def widen_came(part):
        L.f2[part, :] = came[0, part, :].astype(f32)

    row_blocks(seq, seq // 4, widen_came)
    store_other = pltpu.make_async_copy(L.f2, out_x.at[other_rows, :], store_sem.at[2])
    store_other.start()
    store_g.wait()
    for i, part in enumerate(halves):
        swaps[2 + i].wait()
        L.x[part, :] = came[1, part, :].astype(f32)
        copy = pltpu.make_async_copy(L.x.at[part, :], out_g.at[pl.ds(pl.multiple_of((1 - rank) * seq + i * half, 16), half), :], store_sem.at[3 + i])
        copy.start()
        swaps.append(copy)
    store_other.wait()
    for copy in swaps[4:]:
        copy.wait()


INPUTS = ("tokens", "lengths", "wq", "wk", "wv", "wo", "wu", "wd", "mat_a", "mat_b",
          "s_dq", "s_bq", "s_dv", "s_bv", "cotangent")


def on_device(tokens, valid_len, w_query, w_key, w_value, w_out, w_up, w_down, mat_a, mat_b,
              scale_dq, scale_bq, scale_dv, scale_bv, cotangent):
    levels, model, feat = w_query.shape
    hidden, rank_part = w_up.shape[2], mat_a.shape[1]
    ranks = 2
    rows = tokens.shape[0]
    seq = rows // valid_len.shape[0]
    heads = ranks * feat // HEAD_DIM
    bits = (lax.axis_size("batch") - 1).bit_length()
    count = 4 * (2 + 6 * levels)
    shape = jax.ShapeDtypeStruct
    dma = lambda *n: pltpu.SemaphoreType.DMA(n)
    any_spec = pl.BlockSpec(memory_space=pl.ANY)
    vmem_spec = pl.BlockSpec(memory_space=pltpu.VMEM)
    smem_spec = pl.BlockSpec(memory_space=pltpu.SMEM)
    vmem = pltpu.VMEM
    sum_width = 2 * (rank_part + feat)
    outs = dict(
        out_x=shape((rows, model), f32),
        out_g=shape((rows, model), f32),
        out_dq=shape((levels, 1, rank_part), f32),
        out_bq=shape((levels, 1, feat), f32),
        out_dv=shape((levels, 1, rank_part), f32),
        out_bv=shape((levels, 1, feat), f32),
        spill_probs=shape((heads, seq, seq), low),
        spill_att=shape((3, seq, model), low),
        spill_lift=shape((2, seq, model), low),
        spill_inner=shape((seq, ranks * rank_part), low),
        spill_slope=shape((seq, ranks * hidden), low),
    )
    scratch = dict(
        qkv=vmem((levels, 3, model, ranks * feat), low),
        out=vmem((levels, ranks * feat, model), low),
        up=vmem((levels, model, ranks * hidden), low),
        down=vmem((levels, ranks * hidden, model), low),
        full_a=vmem((model, ranks * rank_part), low),
        full_b=vmem((ranks * rank_part, model), low),
        dq=vmem((levels, 1, ranks * rank_part), f32),
        bq=vmem((levels, 1, ranks * feat), f32),
        dv=vmem((levels, 1, ranks * rank_part), f32),
        bv=vmem((levels, 1, ranks * feat), f32),
        bias=vmem((seq, 128), f32),
        x=vmem((seq, model), f32),
        xl=vmem((seq, model), low),
        f2=vmem((seq, model), f32),
        hid=vmem((seq, ranks * hidden), low),
        att=vmem((3, seq, model), low),
        lift=vmem((2, seq, model), low),
        inner=vmem((seq, ranks * rank_part), low),
        probs=vmem((heads, seq, seq), low),
        mix=vmem((seq, model), low),
        normed=vmem((2 * levels, seq, model), low),
        scale=vmem((2 * levels, seq, 1), f32),
        slope=vmem((seq, ranks * hidden), low),
        gone=vmem((seq, model), low),
        came=vmem((2, seq, model), low),
        sum_buf=vmem((levels, 2, 1, sum_width), f32),
        sum_in=vmem((levels, 1 + bits, 1, sum_width), f32),
        load_sem=dma(4 + 6 * levels + 6),
        spill_sem=dma(5),
        small_send=dma(4),
        small_recv=dma(4),
        swap_send=dma(4),
        swap_recv=dma(4),
        sum_send=dma(levels, 1 + bits),
        sum_recv=dma(levels, 1 + bits),
        store_sem=dma(5),
    )
    for i in range(6):
        scratch[f"sem{i}"] = dma(count)
    for i in range(6, 8):
        scratch[f"sem{i}"] = dma(3 * count)
    names = INPUTS + tuple(outs) + tuple(scratch)
    vectors = [v[:, None, :] for v in (scale_dq, scale_bq, scale_dv, scale_bv)]
    macs = seq * model * (5 * ranks * rank_part + 8 * ranks * feat + 4 * ranks * hidden) * levels
    results = pl.pallas_call(
        functools.partial(layers_kernel, levels, names, None),
        out_shape=tuple(outs.values()),
        in_specs=[any_spec, smem_spec] + [any_spec] * 8 + [vmem_spec] * 4 + [any_spec],
        out_specs=(any_spec, any_spec) + (vmem_spec,) * 4 + (any_spec,) * 5,
        scratch_shapes=list(scratch.values()),
        compiler_params=pltpu.CompilerParams(
            collective_id=0, has_side_effects=True, vmem_limit_bytes=64 * 2**20 - 2**18),
        cost_estimate=pl.CostEstimate(flops=2 * macs, bytes_accessed=64 * 2**20, transcendentals=0),
        name="layers",
    )(tokens, valid_len, w_query, w_key, w_value, w_out, w_up, w_down, mat_a, mat_b, *vectors, cotangent)
    return results[:2] + tuple(v[:, 0, :] for v in results[2:6])


def solution(mesh):
    split = P(None, None, "rank")
    down_split = P(None, "rank", None)
    vector = P(None, "rank")
    return jax.shard_map(
        on_device,
        mesh=mesh,
        in_specs=(P("batch", None), P("batch"), split, split, split, down_split, split, down_split,
                  P(None, "rank"), P("rank", None), vector, vector, vector, vector, P("batch", None)),
        out_specs=(P("batch", None), P("batch", None), vector, vector, vector, vector),
        check_vma=False,
    )
```

```python
import functools
import math

import jax
import jax.numpy as jnp
from jax import lax
from jax.experimental import pallas as pl
from jax.experimental.pallas import tpu as pltpu
from jax.sharding import PartitionSpec as P

HEAD_DIM = 64
MESH = pl.DeviceIdType.MESH

epsilon = 1e-05
masked = -1e30

low, f32 = jnp.bfloat16, jnp.float32


def flip(index, bit):
    step = 1 << bit
    return index + step - 2 * step * ((index // step) % 2)


class Exchange:
    LAG = 6
    HOP = 2
    AHEAD = 3

    def __init__(self, groups, loads, sems):
        self.groups, self.loads = groups, loads
        self.sems = {link: sems[2 * i : 2 * i + 2] for i, link in enumerate("yxzc")}
        self.batch = lax.axis_index("batch")
        self.rank = lax.axis_index("rank")
        b = self.batch
        self.core = b % 2
        bit_x, bit_z = (b // 2) % 2, (b // 4) % 2
        self.partner = {
            "y": (b, 1 - self.rank),
            "x": (flip(b, 1), self.rank),
            "z": (flip(b, 2), self.rank),
            "c": (flip(b, 0), self.rank),
        }
        chip = lambda cx, cz: cx + 2 * cz
        own, across, along, far = (
            chip(bit_x, bit_z),
            chip(1 - bit_x, bit_z),
            chip(bit_x, 1 - bit_z),
            chip(1 - bit_x, 1 - bit_z),
        )
        parity = (bit_x + bit_z) % 2
        first = lambda who: 2 * who
        second = lambda who: 2 * who + 1
        pair = lambda par, which: 8 + 2 * par + which
        self.y_units = [first(own), second(own), pair(parity, 0), pair(parity, 1)]
        self.x_units = [first(across), second(across), pair(1 - parity, 0), second(far)]
        self.z_units = [first(along), second(along), first(far), pair(1 - parity, 1)]
        self.x_out = [first(own), second(own), pair(parity, 0), second(along)]
        self.z_out = [first(own), second(own), first(across), pair(parity, 1)]
        self.count = 4 * len(groups)
        self.next_tick = 0
        self.plan()

    def barrier(self):
        bar = pltpu.get_barrier_semaphore()
        for who in self.partner.values():
            pl.semaphore_signal(bar, inc=1, device_id=who, device_id_type=MESH)
        pl.semaphore_wait(bar, len(self.partner))

    def copy(self, src, dst, send, recv, link):
        return pltpu.make_async_remote_copy(
            src_ref=src, dst_ref=dst, send_sem=send, recv_sem=recv,
            device_id=self.partner[link], device_id_type=MESH,
        )

    def move(self, link, item, unit, core, rank):
        ref = self.groups[item // 4].piece(2 * unit + core, rank)
        send, recv = self.sems[link]
        return self.copy(ref, ref, send.at[item // 4], recv.at[item], link)

    def share(self, group, unit, core, rank):
        ref = self.groups[group].piece(2 * unit + core, rank)
        send, recv = self.sems["c"]
        return self.copy(ref, ref, send.at[group], recv.at[group], "c")

    def begin(self, link, item):
        units = {"y": self.y_units, "x": self.x_out, "z": self.z_out}[link]
        self.move(link, item, units[item % 4], self.core, self.rank if link == "y" else 1 - self.rank).start()

    def arrive(self, link, item):
        units = {"y": self.y_units, "x": self.x_units, "z": self.z_units}[link]
        unit = units[item % 4]
        self.move(link, item, unit, self.core, 1 - self.rank).wait_recv()
        self.share(item // 4, unit, self.core, 1 - self.rank).start()

    def sent(self, link, group):
        ref = self.groups[group].many(12 if link == "c" else 4)
        send, recv = self.sems[link]
        self.copy(ref, ref, send.at[group], recv.at[group], link).wait_send()

    def shared(self, group):
        ref = self.groups[group].many(12)
        send, recv = self.sems["c"]
        self.copy(ref, ref, send.at[group], recv.at[group], "c").wait_recv()

    def plan(self):
        lag, hop = self.LAG, self.HOP
        begin = {}
        for item in range(self.count):
            begin["y", item] = item
        for group in range(self.count // 4):
            at = lambda link, j: begin[link, 4 * group + j] + lag
            for link, j in (("x", 0), ("x", 1), ("x", 2), ("z", 0), ("z", 1), ("z", 3)):
                begin[link, 4 * group + j] = at("y", j)
            begin["z", 4 * group + 2] = at("x", 0)
            begin["x", 4 * group + 3] = at("z", 1)
        steps, self.ready = {}, {}
        order = {"y": 0, "x": 1, "z": 2}
        add = lambda tick, *entry: steps.setdefault(tick, []).append(entry)
        for (link, item), tick in begin.items():
            add(tick, 1, order[link], item, "begin", link)
            add(tick + lag, 0, order[link], item, "arrive", link)
            self.ready[item // 4] = max(self.ready.get(item // 4, 0), tick + lag + hop)
        for group, tick in self.ready.items():
            add(tick, 2, 0, group, "shared", "c")
            for link in "yxzc":
                add(tick + lag, 3, 0, group, "sent", link)
        self.steps = {tick: sorted(found) for tick, found in steps.items()}
        self.last_tick = max(steps)

    def tick(self):
        for _, _, item, kind, link in self.steps.get(self.next_tick, []):
            if kind == "begin":
                if link == "y" and item % 4 == 0:
                    for copies in self.loads[item // 4 + self.AHEAD : item // 4 + self.AHEAD + 1]:
                        for copy in copies:
                            copy.start()
                    for copy in self.loads[item // 4]:
                        copy.wait()
                self.begin(link, item)
            elif kind == "arrive":
                self.arrive(link, item)
            elif kind == "shared":
                self.shared(item)
            else:
                self.sent(link, item)
        self.next_tick += 1

    def until(self, group):
        while self.next_tick <= self.ready[group]:
            self.tick()

    def finish(self):
        while self.next_tick <= self.last_tick:
            self.tick()


class Group:
    def __init__(self, piece, many):
        self.piece, self.many = piece, many


def piece_rows(ref, lead, rows, columns):
    height = rows // 24

    def full(piece, rank):
        start = pl.multiple_of(piece * height, 16)
        left = pl.multiple_of(rank * columns, 128)
        return ref.at[(*lead, pl.ds(start, height), pl.ds(left, columns))]

    return Group(full, lambda n: ref.at[(*lead, pl.ds(0, n * height), pl.ds(0, columns))])


def column_groups(ref, lead, rows, columns, parts):
    height, width = rows // 24, columns // parts

    def group(part):
        def full(piece, rank):
            start = pl.multiple_of(piece * height, 16)
            left = pl.multiple_of(rank * columns + part * width, 128)
            return ref.at[(*lead, pl.ds(start, height), pl.ds(left, width))]

        return Group(full, lambda n: ref.at[(*lead, pl.ds(0, n * height), pl.ds(0, width))])

    return [group(part) for part in range(parts)]


def row_groups(ref, lead, rows, parts):
    height = rows // parts // 24

    def group(part):
        def full(piece, rank):
            start = rank * rows + part * (rows // parts) + piece * height
            return ref.at[(*lead, pl.ds(pl.multiple_of(start, 16), height), slice(None))]

        return Group(full, lambda n: ref.at[(*lead, pl.ds(0, n * height), slice(None))])

    return [group(part) for part in range(parts)]


def tile_group(ref, rows, columns):
    height, width = rows // 8, columns // 3

    def full(piece, rank):
        start = pl.multiple_of(rank * rows + (piece % 8) * height, 16)
        left = pl.multiple_of((piece // 8) * width, 128)
        return ref.at[pl.ds(start, height), pl.ds(left, width)]

    return Group(full, lambda n: ref.at[pl.ds(0, n * height), pl.ds(0, width)])


def dot(left, right):
    return jnp.dot(left, right, preferred_element_type=f32)


def dot_back(left, right):
    return lax.dot_general(left, right, (((1,), (1,)), ((), ())), preferred_element_type=f32)


def dot_turned(left, right):
    return lax.dot_general(left, right, (((0,), (0,)), ((), ())), preferred_element_type=f32)


def normalize(values):
    center = values - jnp.mean(values, axis=-1, keepdims=True)
    spread = jnp.mean(center * center, axis=-1, keepdims=True)
    scale = lax.rsqrt(spread + epsilon)
    return center * scale, scale


def normalize_back(grad, normed, scale):
    shared = jnp.mean(grad * normed, axis=-1, keepdims=True)
    return (grad - jnp.mean(grad, axis=-1, keepdims=True) - normed * shared) * scale


def gelu_and_slope(values):
    cdf = 0.5 + 0.5 * lax.erf(values * 0.5**0.5)
    bell = jnp.exp(-0.5 * values * values) * (2.0 * math.pi) ** -0.5
    return values * cdf, cdf + values * bell


def lane_half(shape, which):
    lanes = lax.broadcasted_iota(jnp.int32, shape, 1)
    return (lanes < HEAD_DIM) if which == 0 else (lanes >= HEAD_DIM)


class Layers:
    def __init__(self, refs):
        self.__dict__.update(refs)
        self.rows, self.model = self.x.shape
        self.heads = self.model // HEAD_DIM
        self.ranks = self.full_a.shape[1]
        self.blocks = [pl.ds(start, 64) for start in range(0, self.rows, 64)]

    def vector(self, name, level):
        return getattr(self, name)[level : level + 1, :]

    def adapt(self, level, tick, need):
        ranks = self.ranks
        need("a")
        inner = dot(self.xl[...], self.full_a[...])
        self.inner[...] = inner.astype(low)
        self.hid[:, :ranks] = (inner * self.vector("dq", level)).astype(low)
        self.hid[:, ranks : 2 * ranks] = (inner * self.vector("dv", level)).astype(low)
        tick()
        need("b")
        need("qkv")
        self.att[1] = dot(self.xl[...], self.qkv[level, 1]).astype(low)
        tick()
        for i, (which, scale) in enumerate(((0, "bq"), (2, "bv"))):
            lift = dot(self.hid[:, i * ranks : (i + 1) * ranks], self.full_b[...])
            self.lift[i] = lift.astype(low)
            rows = (dot(self.xl[...], self.qkv[level, which]) + lift * self.vector(scale, level)).astype(low)
            self.att[which] = rows if which else (rows.astype(f32) * HEAD_DIM**-0.5).astype(low)
            tick()

    def attend(self, tick):
        width = 2 * HEAD_DIM
        bias = self.bias[...]
        bias = jnp.concatenate([bias] * (self.rows // bias.shape[1]), axis=1)
        for pair in range(self.heads // 2):
            slab = slice(pair * width, (pair + 1) * width)
            query, keys, values = (self.att[i, :, slab] for i in range(3))
            first = lane_half(query.shape, 0)
            mixed = []
            for which in range(2):
                chosen = jnp.where(first == (which == 0), query, jnp.zeros_like(query))
                scores = dot_back(keys, chosen) + bias
                peak = jnp.max(scores, axis=0, keepdims=True)
                exponent = jnp.exp(scores - peak)
                total = jnp.sum(exponent, axis=0, keepdims=True)
                probs = (exponent * (1.0 / total)).astype(low)
                self.probs[2 * pair + which] = probs
                mixed.append(dot_turned(probs, values))
            self.mix[:, slab] = jnp.where(first, *mixed).astype(low)
            tick()

    def project(self, level, tick, need):
        need("out")
        self.f2[...] = self.x[...] + dot(self.mix[...], self.out[level])
        for part in self.blocks:
            normed, scale = normalize(self.f2[part, :])
            self.f2[part, :] = normed
            self.normed[2 * level, part, :] = normed.astype(low)
            self.scale[2 * level, part, :] = scale
        tick()

    def feed(self, level, rank, tick, need):
        hidden = self.hid.shape[1]
        width = hidden // 6
        for chunk in range(6):
            if chunk == 3:
                need("up0")
            if chunk == 4:
                need("up1")
            columns = pl.ds(pl.multiple_of((rank * 3 + chunk) % 6 * width, 128), width)
            before = dot(self.normed[2 * level], self.up[level, :, columns])
            active, slope = gelu_and_slope(before)
            self.hid[:, columns] = active.astype(low)
            self.slope[:, columns] = slope.astype(low)
            tick()
        half = hidden // 2
        for start, depth, group in ((0, half, None), (half, half // 2, "down0"), (half + half // 2, half // 2, "down1")):
            if group:
                need(group)
            units = pl.ds(pl.multiple_of((rank * half + start) % hidden, 128), depth)
            self.f2[...] += dot(self.hid[:, units], self.down[level, units, :])
            if group != "down1":
                tick()
        for part in self.blocks:
            normed, scale = normalize(self.f2[part, :])
            self.x[part, :] = normed
            self.xl[part, :] = normed.astype(low)
            self.normed[2 * level + 1, part, :] = normed.astype(low)
            self.scale[2 * level + 1, part, :] = scale


    def norm_back(self, index, src):
        for part in self.blocks:
            grad = normalize_back(src[part, :].astype(f32), self.normed[index, part, :].astype(f32), self.scale[index, part, :])
            self.f2[part, :] = grad
            self.xl[part, :] = grad.astype(low)

    def feed_back(self, level, grad, tick):
        self.norm_back(2 * level + 1, grad)
        hidden = self.hid.shape[1]
        width = hidden // 6
        for chunk in range(6):
            columns = slice(chunk * width, (chunk + 1) * width)
            grad = dot_back(self.xl[...], self.down[level, columns, :])
            self.hid[:, columns] = (grad * self.slope[:, columns].astype(f32)).astype(low)
            if chunk % 3 == 2:
                tick()
        self.f2[...] += dot_back(self.hid[...], self.up[level])
        tick()
        self.norm_back(2 * level, self.f2)
        self.mix[...] = dot_back(self.xl[...], self.out[level]).astype(low)
        tick()

    def attend_back(self, tick):
        width = 2 * HEAD_DIM
        for pair in range(self.heads // 2):
            slab = slice(pair * width, (pair + 1) * width)
            query, keys, values = (self.att[i, :, slab] for i in range(3))
            grad = self.mix[:, slab]
            first = lane_half(values.shape, 0)
            grads = [], [], []
            for which in range(2):
                probs = self.probs[2 * pair + which]
                chosen = jnp.where(first == (which == 0), values, jnp.zeros_like(values))
                wide = probs.astype(f32)
                shared = wide * dot_back(chosen, grad)
                delta = jnp.sum(shared, axis=0, keepdims=True)
                dscore = (shared - wide * delta).astype(low)
                grads[0].append(dot_turned(dscore, keys))
                grads[1].append(dot(dscore, query))
                grads[2].append(dot(probs, grad))
            self.att[0, :, slab] = (jnp.where(first, *grads[0]) * HEAD_DIM**-0.5).astype(low)
            self.att[1, :, slab] = jnp.where(first, *grads[1]).astype(low)
            self.att[2, :, slab] = jnp.where(first, *grads[2]).astype(low)
            tick()

    def vectors_back(self, level, part):
        ranks = self.ranks
        total = lambda grid: jnp.sum(grid, axis=0, keepdims=True)
        sums, passed = {}, {}
        for i, (which, scale, name) in enumerate(((0, "bq", "q"), (2, "bv", "v"))):
            rows = self.att[which, part, :].astype(f32)
            sums["b" + name] = total(rows * self.lift[i, part, :].astype(f32))
            passed[name] = slice((1 + i) * ranks, (1 + i) * ranks + self.model)
            self.hid[part, passed[name]] = (rows * self.vector(scale, level)).astype(low)
        found = {"dq": [], "dv": []}
        for columns in (slice(0, ranks // 2), slice(ranks // 2, ranks)):
            inner = self.inner[part, columns].astype(f32)
            grad = 0.0
            for name in ("q", "v"):
                back = dot_back(self.hid[part, passed[name]], self.full_b[columns, :])
                found["d" + name].append(total(back * inner))
                grad += back * self.vector("d" + name, level)[:, columns]
            self.hid[part, columns] = grad.astype(low)
        sums.update({name: jnp.concatenate(pieces, axis=1) for name, pieces in found.items()})
        return sums

    def input_back(self, level, part):
        grad = self.f2[part, :] + dot_back(self.hid[part, : self.ranks], self.full_a[...])
        for i in range(3):
            grad += dot_back(self.att[i, part, :], self.qkv[level, i])
        self.x[part, :] = grad


def layers_kernel(levels, names, groups_of, *refs):
    refs = dict(zip(names, refs))
    get = refs.pop
    ins = [get(n) for n in INPUTS]
    (tokens, lengths, wq, wk, wv, wo, wu, wd, mat_a, mat_b, dq, bq, dv, bv, cotangent) = ins
    rank, batch = lax.axis_index("rank"), lax.axis_index("batch")
    both = refs["x"].shape[0]
    seq = both
    model, feat = wq.shape[1:]
    hidden, rank_part = wu.shape[2], mat_a.shape[1]
    own_x, other_x, own_g, other_g, out_sums = (get(n) for n in ("own_x", "other_x", "own_g", "other_g", "out_sums"))
    spills = [get("spill_probs"), get("spill_att"), get("spill_lift"), get("spill_inner"), get("spill_slope")]
    load_sem, spill_sem, small_send, small_recv = (get(n) for n in ("load_sem", "spill_sem", "small_send", "small_recv"))
    sems = [get(f"sem{i}") for i in range(8)]
    swap_send, swap_recv, sum_send, sum_recv = (get(n) for n in ("swap_send", "swap_recv", "sum_send", "sum_recv"))
    store_sem = get("store_sem")
    gone, came = get("gone"), get("came")
    sum_buf, sum_in = get("sum_buf"), get("sum_in")
    layers = Layers(refs)
    L = layers

    used = [0]

    def load(src, dst):
        copy = pltpu.make_async_copy(src, dst, load_sem.at[used[0]])
        used[0] += 1
        return copy

    def columns_of(size):
        return pl.ds(pl.multiple_of(rank * size, 128), size)

    def rows_of(size):
        return pl.ds(pl.multiple_of(rank * size, 16), size)

    own_rows = rows_of(seq)

    groups, loads, names_of = [], [], {}

    def add(name, found, copies):
        for i, group in enumerate(found):
            names_of[name + (str(i) if len(found) > 1 else "")] = len(groups)
            groups.append(group)
            loads.append(copies if i == 0 else [])

    add("a", [piece_rows(L.full_a, (), model, rank_part)], [load(mat_a, L.full_a.at[:, columns_of(rank_part)])])
    load_x = load(tokens.at[own_rows, :], L.xl)
    add("b", [tile_group(L.full_b, rank_part, model)], [load(mat_b, L.full_b.at[rows_of(rank_part), :])])
    for level in range(levels):
        tag = lambda name: f"{name}/{level}"
        add(f"qkv/{level}", [piece_rows(L.qkv, (level, slice(None)), model, feat)], [
            load(w.at[level], L.qkv.at[level, i, :, columns_of(feat)]) for i, w in enumerate((wq, wk, wv))])
        add(f"out/{level}", row_groups(L.out, (level,), feat, 1), [
            load(wo.at[level], L.out.at[level, rows_of(feat), :])])
        add(f"up/{level}/", column_groups(L.up, (level,), model, hidden, 2), [
            load(wu.at[level], L.up.at[level, :, columns_of(hidden)])])
        add(f"down/{level}/", row_groups(L.down, (level,), hidden, 2), [
            load(wd.at[level], L.down.at[level, rows_of(hidden), :])])
    vectors = [(dq, L.dq), (bq, L.bq), (dv, L.dv), (bv, L.bv)]

    small_loads = [load(src, dst.at[:, columns_of(src.shape[1])]) for src, dst in vectors]
    load_g = load(cotangent.at[own_rows, :], gone)
    exchange = Exchange(groups, loads, sems)
    for copies in (*loads[: exchange.AHEAD], [load_x], small_loads):
        for copy in copies:
            copy.start()
    bits = (lax.axis_size("batch") - 1).bit_length()
    for bit in range(3, bits):
        exchange.partner[bit] = (flip(batch, bit), rank)
    exchange.barrier()
    small = []
    for i, (src, dst) in enumerate(vectors):
        ref = dst.at[:, columns_of(src.shape[1])]
        small.append(exchange.copy(src, ref, small_send.at[i], small_recv.at[i], "y"))
        small[-1].start()

    slots = lax.broadcasted_iota(jnp.int32, L.bias.shape, 0)
    length = lengths[rank]
    L.bias[...] = jnp.where(slots < length, 0.0, masked)

    for _ in range(exchange.LAG):
        exchange.tick()
    load_x.wait()
    load_g.start()

    L.x[...] = L.xl[...].astype(f32)
    for copy in small + small_loads:
        copy.wait()

    spill_src = [L.probs, L.att, L.lift, L.inner, L.slope]
    spill = [pltpu.make_async_copy(src, dst, spill_sem.at[i]) for i, (src, dst) in enumerate(zip(spill_src, spills))]
    fetch = [pltpu.make_async_copy(dst, src, spill_sem.at[i]) for i, (src, dst) in enumerate(zip(spill_src, spills))]
    PROBS, ATT, LIFT, INNER, SLOPE = range(5)

    for level in range(levels):
        def need(name):
            full = {"a": "a", "b": "b", "qkv": f"qkv/{level}", "out": f"out/{level}", "up0": f"up/{level}/0",
                    "up1": f"up/{level}/1", "down0": f"down/{level}/0", "down1": f"down/{level}/1"}[name]
            exchange.until(names_of[full])

        if level:
            for i in (ATT, LIFT, INNER, PROBS):
                spill[i].wait()
        L.adapt(level, exchange.tick, need)
        if not level:
            spill[LIFT].start()
            spill[INNER].start()
        L.attend(exchange.tick)
        if not level:
            spill[ATT].start()
            spill[PROBS].start()
        L.project(level, exchange.tick, need)
        if level:
            spill[SLOPE].wait()
        L.feed(level, rank, exchange.tick, need)
        if not level:
            spill[SLOPE].start()
    exchange.finish()

    def swap(src, index, part, slot):
        return exchange.copy(src.at[part, :], came.at[index, part], swap_send.at[index + slot],
                             swap_recv.at[index + slot], "y")

    first_rows = seq // 4
    store_own = pltpu.make_async_copy(L.x, own_x, store_sem.at[0])
    store_own.start()
    swaps = [swap(L.normed.at[2 * levels - 1], 0, pl.ds(0, seq), 0)]
    swaps[0].start()
    load_g.wait()

    def sum_copy(level, step):
        who = ["y", "c", "x", "z", *range(3, bits)][step]
        src = sum_buf.at[level, 1 - rank] if step == 0 else sum_buf.at[level, rank]
        return exchange.copy(src, sum_in.at[level, step], sum_send.at[level, step], sum_recv.at[level, step], who)

    def sum_step(level, step):
        if step:
            sum_copy(level, step - 1).wait()
            sum_buf[level, rank] += sum_in[level, step - 1]
        if step < 1 + bits:
            sum_copy(level, step).start()

    later = []

    def step_on():
        if later:
            later.pop(0)()

    ORDER = (("dq", rank_part), ("bq", feat), ("dv", rank_part), ("bv", feat))
    for level in reversed(range(levels)):
        last = level == 0
        L.feed_back(level, L.x if level < levels - 1 else gone, step_on)
        if not last:
            fetch[SLOPE].start()
        elif levels > 1:
            fetch[ATT].wait()
            fetch[PROBS].wait()
        L.attend_back(step_on)
        if not last:
            fetch[PROBS].start()
        elif levels > 1:
            fetch[LIFT].wait()
            fetch[INNER].wait()
        if level == levels - 1:
            store_own.wait()
        sums = [{}]
        parts = [pl.ds(0, seq)]
        if last:
            parts = [pl.ds(0, first_rows), pl.ds(first_rows, seq - first_rows)]
        for i, part in enumerate(parts):
            found = L.vectors_back(level, part)
            sums = {name: found[name] + sums[name] if i else found[name] for name in found}
            if i == len(parts) - 1:
                at = 0
                for name, width in ORDER:
                    for side in range(2):
                        sum_buf[level, side, :, pl.ds(at, width)] = sums[name][:, side * width : (side + 1) * width]
                    at += width
                while later:
                    step_on()
                for step in range(2 + bits):
                    later.append(functools.partial(sum_step, level, step))
                step_on()
            L.input_back(level, part)
            if last:
                gone[part, :] = L.x[part, :].astype(low)
                swaps.append(swap(gone, 1, part, i))
                swaps[-1].start()
        if not last:
            for i in (ATT, LIFT, INNER):
                fetch[i].start()
            fetch[SLOPE].wait()
    store_g = pltpu.make_async_copy(L.x, own_g, store_sem.at[1])
    store_g.start()
    swaps[0].wait()
    store_came = [pltpu.make_async_copy(came.at[0], other_x, store_sem.at[2])]
    store_came[0].start()
    while later:
        step_on()
    for level in range(levels):
        out_sums[level : level + 1, :] = sum_buf[level, rank]
    for i, part in enumerate(parts):
        swaps[1 + i].wait()
        store_came.append(pltpu.make_async_copy(came.at[1, part], other_g.at[part, :], store_sem.at[3 + i]))
        store_came[-1].start()
    store_g.wait()
    for copy in store_came:
        copy.wait()


def assemble_kernel(rank_part, feat, own_x, other_x, own_g, other_g, sums, out_x, out_g, *refs):
    out_vectors, (own, came, wide, load_sem, store_sem) = refs[:4], refs[4:]
    rank = lax.axis_index("rank")
    seq = own_x.shape[0]
    half = seq // 2
    place = lambda who, start: pl.ds(pl.multiple_of(who * seq + start, 16), half)
    loads, stores = [], []
    for i, (mine, other) in enumerate(((own_x, other_x), (own_g, other_g))):
        for j in range(2):
            rows = pl.ds(j * half, half)
            for k, (src, dst) in enumerate(((other, came), (mine, own))):
                loads.append(pltpu.make_async_copy(src.at[rows, :], dst.at[i, rows, :], load_sem.at[i, j, k]))
                loads[-1].start()
    for i, out in enumerate((out_x, out_g)):
        for j in range(2):
            rows = pl.ds(j * half, half)
            loads[4 * i + 2 * j].wait()
            wide[i, rows, :] = came[i, rows, :].astype(f32)
            stores.append(pltpu.make_async_copy(wide.at[i, rows, :], out.at[place(1 - rank, j * half), :], store_sem.at[i, j, 0]))
            stores[-1].start()
            loads[4 * i + 2 * j + 1].wait()
            stores.append(pltpu.make_async_copy(own.at[i, rows, :], out.at[place(rank, j * half), :], store_sem.at[i, j, 1]))
            stores[-1].start()
    at = 0
    for width, dst in zip((rank_part, feat, rank_part, feat), out_vectors):
        dst[...] = sums[:, at : at + width]
        at += width
    for copy in stores:
        copy.wait()


INPUTS = ("tokens", "lengths", "wq", "wk", "wv", "wo", "wu", "wd", "mat_a", "mat_b",
          "s_dq", "s_bq", "s_dv", "s_bv", "cotangent")


def on_device(tokens, valid_len, w_query, w_key, w_value, w_out, w_up, w_down, mat_a, mat_b,
              scale_dq, scale_bq, scale_dv, scale_bv, cotangent):
    levels, model, feat = w_query.shape
    hidden, rank_part = w_up.shape[2], mat_a.shape[1]
    ranks = 2
    rows = tokens.shape[0]
    seq = rows // valid_len.shape[0]
    heads = ranks * feat // HEAD_DIM
    bits = (lax.axis_size("batch") - 1).bit_length()
    count = 4 * (2 + 6 * levels)
    shape = jax.ShapeDtypeStruct
    dma = lambda *n: pltpu.SemaphoreType.DMA(n)
    any_spec = pl.BlockSpec(memory_space=pl.ANY)
    vmem_spec = pl.BlockSpec(memory_space=pltpu.VMEM)
    smem_spec = pl.BlockSpec(memory_space=pltpu.SMEM)
    vmem = pltpu.VMEM
    sum_width = 2 * (rank_part + feat)
    outs = dict(
        own_x=shape((seq, model), f32),
        other_x=shape((seq, model), low),
        own_g=shape((seq, model), f32),
        other_g=shape((seq, model), low),
        out_sums=shape((levels, sum_width), f32),
        spill_probs=shape((heads, seq, seq), low),
        spill_att=shape((3, seq, model), low),
        spill_lift=shape((2, seq, model), low),
        spill_inner=shape((seq, ranks * rank_part), low),
        spill_slope=shape((seq, ranks * hidden), low),
    )
    scratch = dict(
        qkv=vmem((levels, 3, model, ranks * feat), low),
        out=vmem((levels, ranks * feat, model), low),
        up=vmem((levels, model, ranks * hidden), low),
        down=vmem((levels, ranks * hidden, model), low),
        full_a=vmem((model, ranks * rank_part), low),
        full_b=vmem((ranks * rank_part, model), low),
        dq=vmem((levels, ranks * rank_part), f32),
        bq=vmem((levels, ranks * feat), f32),
        dv=vmem((levels, ranks * rank_part), f32),
        bv=vmem((levels, ranks * feat), f32),
        bias=vmem((seq, 128), f32),
        x=vmem((seq, model), f32),
        xl=vmem((seq, model), low),
        f2=vmem((seq, model), f32),
        hid=vmem((seq, ranks * hidden), low),
        att=vmem((3, seq, model), low),
        lift=vmem((2, seq, model), low),
        inner=vmem((seq, ranks * rank_part), low),
        probs=vmem((heads, seq, seq), low),
        mix=vmem((seq, model), low),
        normed=vmem((2 * levels, seq, model), low),
        scale=vmem((2 * levels, seq, 1), f32),
        slope=vmem((seq, ranks * hidden), low),
        gone=vmem((seq, model), low),
        came=vmem((2, seq, model), low),
        sum_buf=vmem((levels, 2, 1, sum_width), f32),
        sum_in=vmem((levels, 1 + bits, 1, sum_width), f32),
        load_sem=dma(4 + 6 * levels + 6),
        spill_sem=dma(5),
        small_send=dma(4),
        small_recv=dma(4),
        swap_send=dma(4),
        swap_recv=dma(4),
        sum_send=dma(levels, 1 + bits),
        sum_recv=dma(levels, 1 + bits),
        store_sem=dma(5),
    )
    for i in range(8):
        scratch[f"sem{i}"] = dma(count if i in (1, 3, 5) else count // 4)
    names = INPUTS + tuple(outs) + tuple(scratch)
    vectors = (scale_dq, scale_bq, scale_dv, scale_bv)
    macs = seq * model * (5 * ranks * rank_part + 8 * ranks * feat + 4 * ranks * hidden) * levels
    results = pl.pallas_call(
        functools.partial(layers_kernel, levels, names, None),
        out_shape=tuple(outs.values()),
        in_specs=[any_spec, smem_spec] + [any_spec] * 8 + [vmem_spec] * 4 + [any_spec],
        out_specs=(any_spec,) * 4 + (vmem_spec,) + (any_spec,) * 5,
        scratch_shapes=list(scratch.values()),
        compiler_params=pltpu.CompilerParams(
            collective_id=0, has_side_effects=True, vmem_limit_bytes=64 * 2**20 - 2**18),
        cost_estimate=pl.CostEstimate(flops=2 * macs, bytes_accessed=64 * 2**20, transcendentals=0),
        name="layers",
    )(tokens, valid_len, w_query, w_key, w_value, w_out, w_up, w_down, mat_a, mat_b, *vectors, cotangent)
    return pl.pallas_call(
        functools.partial(assemble_kernel, rank_part, feat),
        out_shape=(shape((rows, model), f32),) * 2
        + tuple(shape((levels, width), f32) for width in (rank_part, feat, rank_part, feat)),
        in_specs=[pl.BlockSpec(memory_space=pltpu.HBM)] * 4 + [vmem_spec],
        out_specs=(any_spec, any_spec) + (vmem_spec,) * 4,
        scratch_shapes=[vmem((2, seq, model), f32), vmem((2, seq, model), low), vmem((2, seq, model), f32),
                        dma(2, 2, 2), dma(2, 2, 2)],
        compiler_params=pltpu.CompilerParams(vmem_limit_bytes=63 * 2**20),
        name="assemble",
    )(*results[:5])


def solution(mesh):
    split = P(None, None, "rank")
    down_split = P(None, "rank", None)
    vector = P(None, "rank")
    return jax.shard_map(
        on_device,
        mesh=mesh,
        in_specs=(P("batch", None), P("batch"), split, split, split, down_split, split, down_split,
                  P(None, "rank"), P("rank", None), vector, vector, vector, vector, P("batch", None)),
        out_specs=(P("batch", None), P("batch", None), vector, vector, vector, vector),
        check_vma=False,
    )
```

```python
import functools
import heapq
import math

import jax
import jax.numpy as jnp
from jax import lax
from jax.experimental import pallas as pl
from jax.experimental.pallas import tpu as pltpu
from jax.sharding import PartitionSpec as P

HEAD_DIM = 64
MESH = pl.DeviceIdType.MESH

epsilon = 1e-05
masked = -1e30

low, f32 = jnp.bfloat16, jnp.float32


def flip(index, bit):
    step = 1 << bit
    return index + step - 2 * step * ((index // step) % 2)


class Exchange:
    LINK, CORE_LINK, LATENCY, CORE_LATENCY, START, WAIT = 45e3, 300e3, 2.6, 1.5, 0.08, 0.03
    LOAD, ENTRY, WINDOW, MARGIN, EARLY = 1.5e6, 8.0, 250e3, 0.2, 1
    AHEAD = 3

    def __init__(self, groups, loads, sems):
        self.groups, self.loads = groups, loads
        self.sems = {link: sems[2 * i : 2 * i + 2] for i, link in enumerate("yxzc")}
        self.batch = lax.axis_index("batch")
        self.rank = lax.axis_index("rank")
        b = self.batch
        self.core = b % 2
        bit_x, bit_z = (b // 2) % 2, (b // 4) % 2
        self.partner = {
            "y": (b, 1 - self.rank),
            "x": (flip(b, 1), self.rank),
            "z": (flip(b, 2), self.rank),
            "c": (flip(b, 0), self.rank),
        }
        chip = lambda cx, cz: cx + 2 * cz
        own, across, along, far = (
            chip(bit_x, bit_z),
            chip(1 - bit_x, bit_z),
            chip(bit_x, 1 - bit_z),
            chip(1 - bit_x, 1 - bit_z),
        )
        parity = (bit_x + bit_z) % 2
        first = lambda who: 2 * who
        second = lambda who: 2 * who + 1
        pair = lambda par, which: 8 + 2 * par + which
        self.y_units = [first(own), second(own), pair(parity, 0), pair(parity, 1)]
        self.x_units = [first(across), second(across), pair(1 - parity, 0), second(far)]
        self.z_units = [first(along), second(along), first(far), pair(1 - parity, 1)]
        self.x_out = [first(own), second(own), pair(parity, 0), second(along)]
        self.z_out = [first(own), second(own), first(across), pair(parity, 1)]
        self.count = 4 * len(groups)
        self.next_tick = 0
        self.here = set()

    def barrier(self):
        bar = pltpu.get_barrier_semaphore()
        for who in self.partner.values():
            pl.semaphore_signal(bar, inc=1, device_id=who, device_id_type=MESH)
        pl.semaphore_wait(bar, len(self.partner))

    def copy(self, src, dst, send, recv, link):
        return pltpu.make_async_remote_copy(
            src_ref=src, dst_ref=dst, send_sem=send, recv_sem=recv,
            device_id=self.partner[link], device_id_type=MESH,
        )

    def move(self, link, item, unit, core, rank):
        ref = self.groups[item // 4].piece(2 * unit + core, rank)
        send, recv = self.sems[link]
        return self.copy(ref, ref, send.at[item // 4], recv.at[item], link)

    def share(self, group, unit, core, rank):
        ref = self.groups[group].piece(2 * unit + core, rank)
        send, recv = self.sems["c"]
        return self.copy(ref, ref, send.at[group], recv.at[group], "c")

    def begin(self, link, item):
        units = {"y": self.y_units, "x": self.x_out, "z": self.z_out}[link]
        self.move(link, item, units[item % 4], self.core, self.rank if link == "y" else 1 - self.rank).start()

    def arrive(self, link, item):
        units = {"y": self.y_units, "x": self.x_units, "z": self.z_units}[link]
        unit = units[item % 4]
        self.move(link, item, unit, self.core, 1 - self.rank).wait_recv()
        self.share(item // 4, unit, self.core, 1 - self.rank).start()

    def sent(self, link, group):
        ref = self.groups[group].many(12 if link == "c" else 4)
        send, recv = self.sems[link]
        self.copy(ref, ref, send.at[group], recv.at[group], link).wait_send()

    def shared(self, group):
        ref = self.groups[group].many(12)
        send, recv = self.sems["c"]
        self.copy(ref, ref, send.at[group], recv.at[group], "c").wait_recv()

    def plan(self, steps):
        size = [group.bytes for group in self.groups]
        now = self.ENTRY
        loaded, at = [], self.ENTRY - 4.0
        for bytes_ in size:
            at += 24 * bytes_ / self.LOAD
            loaded.append(at)
        queue = []
        for group in range(len(size) + self.EARLY):
            if group < len(size):
                queue += [4 * group, 4 * group + 1]
            if group >= self.EARLY:
                queue += [4 * (group - self.EARLY) + 2, 4 * (group - self.EARLY) + 3]
        free = dict.fromkeys("yxzc", 0.0)
        pending, arrived, here, batches, batch = [], {}, {}, [], []

        def send(link, item):
            nonlocal now
            now += self.START
            rate, latency = (self.CORE_LINK, self.CORE_LATENCY) if link == "c" else (self.LINK, self.LATENCY)
            free[link] = max(now, free[link]) + size[item // 4] / rate
            heapq.heappush(pending, (free[link] + latency, len(batches), len(batch), link, item))
            if link != "c":
                batch.append(("begin", link, item))

        def supply():
            while queue:
                item = queue[0]
                behind = max(0.0, free["y"] - now) * self.LINK
                if behind > 1 and behind + size[item // 4] > self.WINDOW or loaded[item // 4] > now:
                    break
                queue.pop(0)
                send("y", item)

        def serve():
            nonlocal now
            supply()
            while pending and pending[0][0] + self.MARGIN <= now:
                *_, link, item = heapq.heappop(pending)
                group, j = divmod(item, 4)
                now += self.WAIT
                if link == "c":
                    here[group] = here.get(group, 0) + 1
                    if here[group] == 12:
                        batch.append(("shared", link, group))
                else:
                    batch.append(("arrive", link, item))
                    if link == "y":
                        for onward in (("x", "z"), ("x", "z"), ("x",), ("z",))[j]:
                            send(onward, item)
                    elif (link, j) == ("x", 0):
                        send("z", 4 * group + 2)
                    elif (link, j) == ("z", 1):
                        send("x", 4 * group + 3)
                    send("c", item)
                supply()

        def pause():
            nonlocal now
            after = [pending[0][0] + self.MARGIN] if pending else []
            if queue:
                item = queue[0]
                room = free["y"] - max(0.0, self.WINDOW - size[item // 4]) / self.LINK
                after.append(max(loaded[item // 4], room))
            now = max(now + 0.02, min(after))

        for length, needed in steps:
            serve()
            while any(here.get(group, 0) < 12 for group in needed):
                pause()
                serve()
            batches.append(batch)
            batch = []
            now += length
        while queue or pending:
            pause()
            serve()
        batches.append(batch)
        self.batches = batches

    def tick(self):
        for kind, link, item in self.batches[self.next_tick]:
            if kind == "begin":
                if link == "y" and item % 4 == 0:
                    for copies in self.loads[item // 4 + self.AHEAD : item // 4 + self.AHEAD + 1]:
                        for copy in copies:
                            copy.start()
                    for copy in self.loads[item // 4]:
                        copy.wait()
                self.begin(link, item)
            elif kind == "arrive":
                self.arrive(link, item)
            else:
                self.shared(item)
                self.here.add(item)
        self.next_tick += 1

    def settle(self):
        for group in range(len(self.groups)):
            for link in "yxzc":
                self.sent(link, group)


class Group:
    def __init__(self, piece, many):
        self.piece, self.many = piece, many
        shape = many(1).shape
        self.bytes = math.prod(shape) * 2


def piece_rows(ref, lead, rows, columns):
    height = rows // 24

    def full(piece, rank):
        start = pl.multiple_of(piece * height, 16)
        left = pl.multiple_of(rank * columns, 128)
        return ref.at[(*lead, pl.ds(start, height), pl.ds(left, columns))]

    return Group(full, lambda n: ref.at[(*lead, pl.ds(0, n * height), pl.ds(0, columns))])


def column_groups(ref, lead, rows, columns, parts):
    height, width = rows // 24, columns // parts

    def group(part):
        def full(piece, rank):
            start = pl.multiple_of(piece * height, 16)
            left = pl.multiple_of(rank * columns + part * width, 128)
            return ref.at[(*lead, pl.ds(start, height), pl.ds(left, width))]

        return Group(full, lambda n: ref.at[(*lead, pl.ds(0, n * height), pl.ds(0, width))])

    return [group(part) for part in range(parts)]


def row_groups(ref, lead, rows, parts):
    height = rows // parts // 24

    def group(part):
        def full(piece, rank):
            start = rank * rows + part * (rows // parts) + piece * height
            return ref.at[(*lead, pl.ds(pl.multiple_of(start, 16), height), slice(None))]

        return Group(full, lambda n: ref.at[(*lead, pl.ds(0, n * height), slice(None))])

    return [group(part) for part in range(parts)]


def tile_group(ref, rows, columns):
    height, width = rows // 8, columns // 3

    def full(piece, rank):
        start = pl.multiple_of(rank * rows + (piece % 8) * height, 16)
        left = pl.multiple_of((piece // 8) * width, 128)
        return ref.at[pl.ds(start, height), pl.ds(left, width)]

    return Group(full, lambda n: ref.at[pl.ds(0, n * height), pl.ds(0, width)])


def dot(left, right):
    return jnp.dot(left, right, preferred_element_type=f32)


def dot_back(left, right):
    return lax.dot_general(left, right, (((1,), (1,)), ((), ())), preferred_element_type=f32)


def dot_turned(left, right):
    return lax.dot_general(left, right, (((0,), (0,)), ((), ())), preferred_element_type=f32)


def normalize(values):
    center = values - jnp.mean(values, axis=-1, keepdims=True)
    spread = jnp.mean(center * center, axis=-1, keepdims=True)
    scale = lax.rsqrt(spread + epsilon)
    return center * scale, scale


def normalize_back(grad, normed, scale):
    shared = jnp.mean(grad * normed, axis=-1, keepdims=True)
    return (grad - jnp.mean(grad, axis=-1, keepdims=True) - normed * shared) * scale


def gelu_and_slope(values):
    cdf = 0.5 + 0.5 * lax.erf(values * 0.5**0.5)
    bell = jnp.exp(-0.5 * values * values) * (2.0 * math.pi) ** -0.5
    return values * cdf, cdf + values * bell


def lane_half(shape, which):
    lanes = lax.broadcasted_iota(jnp.int32, shape, 1)
    return (lanes < HEAD_DIM) if which == 0 else (lanes >= HEAD_DIM)


class Layers:
    def __init__(self, refs):
        self.__dict__.update(refs)
        self.rows, self.model = self.x.shape
        self.heads = self.model // HEAD_DIM
        self.ranks = self.full_a.shape[1]
        self.blocks = [pl.ds(start, 64) for start in range(0, self.rows, 64)]

    def vector(self, name, level):
        return getattr(self, name)[level : level + 1, :]

    def adapt(self, level, tick, need):
        ranks = self.ranks
        tick()
        need("a")
        inner = dot(self.xl[...], self.full_a[...])
        self.inner[...] = inner.astype(low)
        self.hid[:, :ranks] = (inner * self.vector("dq", level)).astype(low)
        self.hid[:, ranks : 2 * ranks] = (inner * self.vector("dv", level)).astype(low)
        tick()
        need("b")
        need("qkv")
        self.att[1] = dot(self.xl[...], self.qkv[level, 1]).astype(low)
        for i, (which, scale) in enumerate(((0, "bq"), (2, "bv"))):
            tick()
            lift = dot(self.hid[:, i * ranks : (i + 1) * ranks], self.full_b[...])
            self.lift[i] = lift.astype(low)
            rows = (dot(self.xl[...], self.qkv[level, which]) + lift * self.vector(scale, level)).astype(low)
            self.att[which] = rows if which else (rows.astype(f32) * HEAD_DIM**-0.5).astype(low)

    def attend(self, tick):
        width = 2 * HEAD_DIM
        bias = self.bias[...]
        bias = jnp.concatenate([bias] * (self.rows // bias.shape[1]), axis=1)
        for pair in range(self.heads // 2):
            tick()
            slab = slice(pair * width, (pair + 1) * width)
            query, keys, values = (self.att[i, :, slab] for i in range(3))
            first = lane_half(query.shape, 0)
            mixed = []
            for which in range(2):
                chosen = jnp.where(first == (which == 0), query, jnp.zeros_like(query))
                scores = dot_back(keys, chosen) + bias
                peak = jnp.max(scores, axis=0, keepdims=True)
                exponent = jnp.exp(scores - peak)
                total = jnp.sum(exponent, axis=0, keepdims=True)
                probs = (exponent * (1.0 / total)).astype(low)
                self.probs[2 * pair + which] = probs
                mixed.append(dot_turned(probs, values))
            self.mix[:, slab] = jnp.where(first, *mixed).astype(low)

    def project(self, level, tick, need):
        tick()
        need("out")
        self.f2[...] = self.x[...] + dot(self.mix[...], self.out[level])
        for part in self.blocks:
            normed, scale = normalize(self.f2[part, :])
            self.f2[part, :] = normed
            self.normed[2 * level, part, :] = normed.astype(low)
            self.scale[2 * level, part, :] = scale

    def feed(self, level, rank, tick, need):
        hidden = self.hid.shape[1]
        width = hidden // 6
        for chunk in range(6):
            tick()
            if chunk == 3:
                need("up")
            columns = pl.ds(pl.multiple_of((rank * 3 + chunk) % 6 * width, 128), width)
            before = dot(self.normed[2 * level], self.up[level, :, columns])
            active, slope = gelu_and_slope(before)
            self.hid[:, columns] = active.astype(low)
            self.slope[:, columns] = slope.astype(low)
        half = hidden // 2
        for start, group in ((0, None), (half, "down")):
            tick()
            if group:
                need(group)
            units = pl.ds(pl.multiple_of((rank * half + start) % hidden, 128), half)
            self.f2[...] += dot(self.hid[:, units], self.down[level, units, :])
        for part in self.blocks:
            normed, scale = normalize(self.f2[part, :])
            self.x[part, :] = normed
            self.xl[part, :] = normed.astype(low)
            self.normed[2 * level + 1, part, :] = normed.astype(low)
            self.scale[2 * level + 1, part, :] = scale


    def norm_back(self, index, src):
        for part in self.blocks:
            grad = normalize_back(src[part, :].astype(f32), self.normed[index, part, :].astype(f32), self.scale[index, part, :])
            self.f2[part, :] = grad
            self.xl[part, :] = grad.astype(low)

    def feed_back(self, level, grad, tick):
        self.norm_back(2 * level + 1, grad)
        hidden = self.hid.shape[1]
        width = hidden // 6
        for chunk in range(6):
            columns = slice(chunk * width, (chunk + 1) * width)
            grad = dot_back(self.xl[...], self.down[level, columns, :])
            self.hid[:, columns] = (grad * self.slope[:, columns].astype(f32)).astype(low)
            if chunk % 3 == 2:
                tick()
        self.f2[...] += dot_back(self.hid[...], self.up[level])
        tick()
        self.norm_back(2 * level, self.f2)
        self.mix[...] = dot_back(self.xl[...], self.out[level]).astype(low)
        tick()

    def attend_back(self, tick):
        width = 2 * HEAD_DIM
        for pair in range(self.heads // 2):
            slab = slice(pair * width, (pair + 1) * width)
            query, keys, values = (self.att[i, :, slab] for i in range(3))
            grad = self.mix[:, slab]
            first = lane_half(values.shape, 0)
            grads = [], [], []
            for which in range(2):
                probs = self.probs[2 * pair + which]
                chosen = jnp.where(first == (which == 0), values, jnp.zeros_like(values))
                wide = probs.astype(f32)
                shared = wide * dot_back(chosen, grad)
                delta = jnp.sum(shared, axis=0, keepdims=True)
                dscore = (shared - wide * delta).astype(low)
                grads[0].append(dot_turned(dscore, keys))
                grads[1].append(dot(dscore, query))
                grads[2].append(dot(probs, grad))
            self.att[0, :, slab] = (jnp.where(first, *grads[0]) * HEAD_DIM**-0.5).astype(low)
            self.att[1, :, slab] = jnp.where(first, *grads[1]).astype(low)
            self.att[2, :, slab] = jnp.where(first, *grads[2]).astype(low)
            tick()

    def vectors_back(self, level, part):
        ranks = self.ranks
        total = lambda grid: jnp.sum(grid, axis=0, keepdims=True)
        sums, passed = {}, {}
        for i, (which, scale, name) in enumerate(((0, "bq", "q"), (2, "bv", "v"))):
            rows = self.att[which, part, :].astype(f32)
            sums["b" + name] = total(rows * self.lift[i, part, :].astype(f32))
            passed[name] = slice((1 + i) * ranks, (1 + i) * ranks + self.model)
            self.hid[part, passed[name]] = (rows * self.vector(scale, level)).astype(low)
        found = {"dq": [], "dv": []}
        for columns in (slice(0, ranks // 2), slice(ranks // 2, ranks)):
            inner = self.inner[part, columns].astype(f32)
            grad = 0.0
            for name in ("q", "v"):
                back = dot_back(self.hid[part, passed[name]], self.full_b[columns, :])
                found["d" + name].append(total(back * inner))
                grad += back * self.vector("d" + name, level)[:, columns]
            self.hid[part, columns] = grad.astype(low)
        sums.update({name: jnp.concatenate(pieces, axis=1) for name, pieces in found.items()})
        return sums

    def input_back(self, level, part):
        grad = self.f2[part, :] + dot_back(self.hid[part, : self.ranks], self.full_a[...])
        for i in range(3):
            grad += dot_back(self.att[i, part, :], self.qkv[level, i])
        self.x[part, :] = grad


def layers_kernel(levels, names, groups_of, *refs):
    refs = dict(zip(names, refs))
    get = refs.pop
    ins = [get(n) for n in INPUTS]
    (tokens, lengths, wq, wk, wv, wo, wu, wd, mat_a, mat_b, dq, bq, dv, bv, cotangent) = ins
    rank, batch = lax.axis_index("rank"), lax.axis_index("batch")
    both = refs["x"].shape[0]
    seq = both
    model, feat = wq.shape[1:]
    hidden, rank_part = wu.shape[2], mat_a.shape[1]
    own_x, other_x, own_g, other_g, out_sums = (get(n) for n in ("own_x", "other_x", "own_g", "other_g", "out_sums"))
    spills = [get("spill_probs"), get("spill_att"), get("spill_lift"), get("spill_inner"), get("spill_slope")]
    load_sem, spill_sem, small_send, small_recv = (get(n) for n in ("load_sem", "spill_sem", "small_send", "small_recv"))
    sems = [get(f"sem{i}") for i in range(8)]
    swap_send, swap_recv, sum_send, sum_recv = (get(n) for n in ("swap_send", "swap_recv", "sum_send", "sum_recv"))
    store_sem = get("store_sem")
    gone, came = get("gone"), get("came")
    sum_buf, sum_in = get("sum_buf"), get("sum_in")
    layers = Layers(refs)
    L = layers

    used = [0]

    def load(src, dst):
        copy = pltpu.make_async_copy(src, dst, load_sem.at[used[0]])
        used[0] += 1
        return copy

    def columns_of(size):
        return pl.ds(pl.multiple_of(rank * size, 128), size)

    def rows_of(size):
        return pl.ds(pl.multiple_of(rank * size, 16), size)

    own_rows = rows_of(seq)

    groups, loads, names_of = [], [], {}

    def add(name, found, copies):
        for i, group in enumerate(found):
            names_of[name + (str(i) if len(found) > 1 else "")] = len(groups)
            groups.append(group)
            loads.append(copies if i == 0 else [])

    add("a", [piece_rows(L.full_a, (), model, rank_part)], [load(mat_a, L.full_a.at[:, columns_of(rank_part)])])
    load_x = load(tokens.at[own_rows, :], L.xl)
    add("b", [tile_group(L.full_b, rank_part, model)], [load(mat_b, L.full_b.at[rows_of(rank_part), :])])
    for level in range(levels):
        add(f"qkv/{level}", [piece_rows(L.qkv, (level, slice(None)), model, feat)], [
            load(w.at[level], L.qkv.at[level, i, :, columns_of(feat)]) for i, w in enumerate((wq, wk, wv))])
        add(f"out/{level}", row_groups(L.out, (level,), feat, 1), [
            load(wo.at[level], L.out.at[level, rows_of(feat), :])])
        add(f"up/{level}", column_groups(L.up, (level,), model, hidden, 1), [
            load(wu.at[level], L.up.at[level, :, columns_of(hidden)])])
        add(f"down/{level}", row_groups(L.down, (level,), hidden, 1), [
            load(wd.at[level], L.down.at[level, rows_of(hidden), :])])
    vectors = [(dq, L.dq), (bq, L.bq), (dv, L.dv), (bv, L.bv)]

    small_loads = [load(src, dst.at[:, columns_of(src.shape[1])]) for src, dst in vectors]
    load_g = load(cotangent.at[own_rows, :], gone)
    exchange = Exchange(groups, loads, sems)
    for copies in (*loads[: exchange.AHEAD], [load_x], small_loads):
        for copy in copies:
            copy.start()
    bits = (lax.axis_size("batch") - 1).bit_length()
    for bit in range(3, bits):
        exchange.partner[bit] = (flip(batch, bit), rank)
    exchange.barrier()
    small = []
    for i, (src, dst) in enumerate(vectors):
        ref = dst.at[:, columns_of(src.shape[1])]
        small.append(exchange.copy(src, ref, small_send.at[i], small_recv.at[i], "y"))
        small[-1].start()

    slots = lax.broadcasted_iota(jnp.int32, L.bias.shape, 0)
    length = lengths[rank]
    L.bias[...] = jnp.where(slots < length, 0.0, masked)

    steps = []
    for level in range(levels):
        at = lambda name: [names_of[f"{name}/{level}"]]
        steps += [(1.3, [names_of["a"]]), (0.75, [names_of["b"]] + at("qkv")), (1.2, []), (1.2, [])]
        steps += [(0.86, [])] * (L.heads // 2) + [(1.0, at("out"))]
        steps += [(0.42, at("up") if chunk == 3 else []) for chunk in range(6)]
        steps += [(1.3, []), (1.8, at("down"))]
    exchange.plan(steps)
    load_x.wait()

    L.x[...] = L.xl[...].astype(f32)
    for copy in small + small_loads:
        copy.wait()

    spill_src = [L.probs, L.att, L.lift, L.inner, L.slope]
    spill = [pltpu.make_async_copy(src, dst, spill_sem.at[i]) for i, (src, dst) in enumerate(zip(spill_src, spills))]
    fetch = [pltpu.make_async_copy(dst, src, spill_sem.at[i]) for i, (src, dst) in enumerate(zip(spill_src, spills))]
    PROBS, ATT, LIFT, INNER, SLOPE = range(5)

    for level in range(levels):
        def need(name):
            assert names_of[name if name in "ab" else f"{name}/{level}"] in exchange.here

        if level:
            for i in (ATT, LIFT, INNER, PROBS):
                spill[i].wait()
        L.adapt(level, exchange.tick, need)
        if not level:
            spill[LIFT].start()
            spill[INNER].start()
        L.attend(exchange.tick)
        if not level:
            spill[ATT].start()
            spill[PROBS].start()
        L.project(level, exchange.tick, need)
        if level:
            spill[SLOPE].wait()
        L.feed(level, rank, exchange.tick, need)
        if not level:
            spill[SLOPE].start()
    exchange.tick()
    load_g.start()

    def swap(src, index, part, slot):
        return exchange.copy(src.at[part, :], came.at[index, part], swap_send.at[index + slot],
                             swap_recv.at[index + slot], "y")

    first_rows = seq // 4
    store_own = pltpu.make_async_copy(L.x, own_x, store_sem.at[0])
    store_own.start()
    swaps = [swap(L.normed.at[2 * levels - 1], 0, pl.ds(0, seq), 0)]
    swaps[0].start()
    load_g.wait()

    def sum_copy(level, step):
        who = ["y", "c", "x", "z", *range(3, bits)][step]
        src = sum_buf.at[level, 1 - rank] if step == 0 else sum_buf.at[level, rank]
        return exchange.copy(src, sum_in.at[level, step], sum_send.at[level, step], sum_recv.at[level, step], who)

    def sum_step(level, step):
        if step:
            sum_copy(level, step - 1).wait()
            sum_buf[level, rank] += sum_in[level, step - 1]
        if step < 1 + bits:
            sum_copy(level, step).start()

    later = []

    def step_on():
        if later:
            later.pop(0)()

    ORDER = (("dq", rank_part), ("bq", feat), ("dv", rank_part), ("bv", feat))
    for level in reversed(range(levels)):
        last = level == 0
        L.feed_back(level, L.x if level < levels - 1 else gone, step_on)
        if not last:
            fetch[SLOPE].start()
        elif levels > 1:
            fetch[ATT].wait()
            fetch[PROBS].wait()
        L.attend_back(step_on)
        if not last:
            fetch[PROBS].start()
        elif levels > 1:
            fetch[LIFT].wait()
            fetch[INNER].wait()
        if level == levels - 1:
            store_own.wait()
        sums = [{}]
        parts = [pl.ds(0, seq)]
        if last:
            parts = [pl.ds(0, first_rows), pl.ds(first_rows, seq - first_rows)]
        for i, part in enumerate(parts):
            found = L.vectors_back(level, part)
            sums = {name: found[name] + sums[name] if i else found[name] for name in found}
            if i == len(parts) - 1:
                at = 0
                for name, width in ORDER:
                    for side in range(2):
                        sum_buf[level, side, :, pl.ds(at, width)] = sums[name][:, side * width : (side + 1) * width]
                    at += width
                while later:
                    step_on()
                for step in range(2 + bits):
                    later.append(functools.partial(sum_step, level, step))
                step_on()
            L.input_back(level, part)
            if last:
                gone[part, :] = L.x[part, :].astype(low)
                swaps.append(swap(gone, 1, part, i))
                swaps[-1].start()
        if not last:
            for i in (ATT, LIFT, INNER):
                fetch[i].start()
            fetch[SLOPE].wait()
    store_g = pltpu.make_async_copy(L.x, own_g, store_sem.at[1])
    store_g.start()
    exchange.settle()
    swaps[0].wait()
    store_came = [pltpu.make_async_copy(came.at[0], other_x, store_sem.at[2])]
    store_came[0].start()
    while later:
        step_on()
    for level in range(levels):
        out_sums[level : level + 1, :] = sum_buf[level, rank]
    for i, part in enumerate(parts):
        swaps[1 + i].wait()
        store_came.append(pltpu.make_async_copy(came.at[1, part], other_g.at[part, :], store_sem.at[3 + i]))
        store_came[-1].start()
    store_g.wait()
    for copy in store_came:
        copy.wait()


def assemble_kernel(rank_part, feat, own_x, other_x, own_g, other_g, sums, out_x, out_g, *refs):
    out_vectors, (own, came, wide, load_sem, store_sem) = refs[:4], refs[4:]
    rank = lax.axis_index("rank")
    seq = own_x.shape[0]
    half = seq // 2
    place = lambda who, start: pl.ds(pl.multiple_of(who * seq + start, 16), half)
    loads, stores = [], []
    for i, (mine, other) in enumerate(((own_x, other_x), (own_g, other_g))):
        for j in range(2):
            rows = pl.ds(j * half, half)
            for k, (src, dst) in enumerate(((other, came), (mine, own))):
                loads.append(pltpu.make_async_copy(src.at[rows, :], dst.at[i, rows, :], load_sem.at[i, j, k]))
                loads[-1].start()
    for i, out in enumerate((out_x, out_g)):
        for j in range(2):
            rows = pl.ds(j * half, half)
            loads[4 * i + 2 * j].wait()
            wide[i, rows, :] = came[i, rows, :].astype(f32)
            stores.append(pltpu.make_async_copy(wide.at[i, rows, :], out.at[place(1 - rank, j * half), :], store_sem.at[i, j, 0]))
            stores[-1].start()
            loads[4 * i + 2 * j + 1].wait()
            stores.append(pltpu.make_async_copy(own.at[i, rows, :], out.at[place(rank, j * half), :], store_sem.at[i, j, 1]))
            stores[-1].start()
    at = 0
    for width, dst in zip((rank_part, feat, rank_part, feat), out_vectors):
        dst[...] = sums[:, at : at + width]
        at += width
    for copy in stores:
        copy.wait()


INPUTS = ("tokens", "lengths", "wq", "wk", "wv", "wo", "wu", "wd", "mat_a", "mat_b",
          "s_dq", "s_bq", "s_dv", "s_bv", "cotangent")


def on_device(tokens, valid_len, w_query, w_key, w_value, w_out, w_up, w_down, mat_a, mat_b,
              scale_dq, scale_bq, scale_dv, scale_bv, cotangent):
    levels, model, feat = w_query.shape
    hidden, rank_part = w_up.shape[2], mat_a.shape[1]
    ranks = 2
    rows = tokens.shape[0]
    seq = rows // valid_len.shape[0]
    heads = ranks * feat // HEAD_DIM
    bits = (lax.axis_size("batch") - 1).bit_length()
    count = 4 * (2 + 4 * levels)
    shape = jax.ShapeDtypeStruct
    dma = lambda *n: pltpu.SemaphoreType.DMA(n)
    any_spec = pl.BlockSpec(memory_space=pl.ANY)
    vmem_spec = pl.BlockSpec(memory_space=pltpu.VMEM)
    smem_spec = pl.BlockSpec(memory_space=pltpu.SMEM)
    vmem = pltpu.VMEM
    sum_width = 2 * (rank_part + feat)
    outs = dict(
        own_x=shape((seq, model), f32),
        other_x=shape((seq, model), low),
        own_g=shape((seq, model), f32),
        other_g=shape((seq, model), low),
        out_sums=shape((levels, sum_width), f32),
        spill_probs=shape((heads, seq, seq), low),
        spill_att=shape((3, seq, model), low),
        spill_lift=shape((2, seq, model), low),
        spill_inner=shape((seq, ranks * rank_part), low),
        spill_slope=shape((seq, ranks * hidden), low),
    )
    scratch = dict(
        qkv=vmem((levels, 3, model, ranks * feat), low),
        out=vmem((levels, ranks * feat, model), low),
        up=vmem((levels, model, ranks * hidden), low),
        down=vmem((levels, ranks * hidden, model), low),
        full_a=vmem((model, ranks * rank_part), low),
        full_b=vmem((ranks * rank_part, model), low),
        dq=vmem((levels, ranks * rank_part), f32),
        bq=vmem((levels, ranks * feat), f32),
        dv=vmem((levels, ranks * rank_part), f32),
        bv=vmem((levels, ranks * feat), f32),
        bias=vmem((seq, 128), f32),
        x=vmem((seq, model), f32),
        xl=vmem((seq, model), low),
        f2=vmem((seq, model), f32),
        hid=vmem((seq, ranks * hidden), low),
        att=vmem((3, seq, model), low),
        lift=vmem((2, seq, model), low),
        inner=vmem((seq, ranks * rank_part), low),
        probs=vmem((heads, seq, seq), low),
        mix=vmem((seq, model), low),
        normed=vmem((2 * levels, seq, model), low),
        scale=vmem((2 * levels, seq, 1), f32),
        slope=vmem((seq, ranks * hidden), low),
        gone=vmem((seq, model), low),
        came=vmem((2, seq, model), low),
        sum_buf=vmem((levels, 2, 1, sum_width), f32),
        sum_in=vmem((levels, 1 + bits, 1, sum_width), f32),
        load_sem=dma(4 + 6 * levels + 6),
        spill_sem=dma(5),
        small_send=dma(4),
        small_recv=dma(4),
        swap_send=dma(4),
        swap_recv=dma(4),
        sum_send=dma(levels, 1 + bits),
        sum_recv=dma(levels, 1 + bits),
        store_sem=dma(5),
    )
    for i in range(8):
        scratch[f"sem{i}"] = dma(count if i in (1, 3, 5) else count // 4)
    names = INPUTS + tuple(outs) + tuple(scratch)
    vectors = (scale_dq, scale_bq, scale_dv, scale_bv)
    macs = seq * model * (5 * ranks * rank_part + 8 * ranks * feat + 4 * ranks * hidden) * levels
    results = pl.pallas_call(
        functools.partial(layers_kernel, levels, names, None),
        out_shape=tuple(outs.values()),
        in_specs=[any_spec, smem_spec] + [any_spec] * 8 + [vmem_spec] * 4 + [any_spec],
        out_specs=(any_spec,) * 4 + (vmem_spec,) + (any_spec,) * 5,
        scratch_shapes=list(scratch.values()),
        compiler_params=pltpu.CompilerParams(
            collective_id=0, has_side_effects=True, vmem_limit_bytes=64 * 2**20 - 2**18),
        cost_estimate=pl.CostEstimate(flops=2 * macs, bytes_accessed=64 * 2**20, transcendentals=0),
        name="layers",
    )(tokens, valid_len, w_query, w_key, w_value, w_out, w_up, w_down, mat_a, mat_b, *vectors, cotangent)
    return pl.pallas_call(
        functools.partial(assemble_kernel, rank_part, feat),
        out_shape=(shape((rows, model), f32),) * 2
        + tuple(shape((levels, width), f32) for width in (rank_part, feat, rank_part, feat)),
        in_specs=[pl.BlockSpec(memory_space=pltpu.HBM)] * 4 + [vmem_spec],
        out_specs=(any_spec, any_spec) + (vmem_spec,) * 4,
        scratch_shapes=[vmem((2, seq, model), f32), vmem((2, seq, model), low), vmem((2, seq, model), f32),
                        dma(2, 2, 2), dma(2, 2, 2)],
        compiler_params=pltpu.CompilerParams(vmem_limit_bytes=63 * 2**20),
        name="assemble",
    )(*results[:5])


def solution(mesh):
    split = P(None, None, "rank")
    down_split = P(None, "rank", None)
    vector = P(None, "rank")
    return jax.shard_map(
        on_device,
        mesh=mesh,
        in_specs=(P("batch", None), P("batch"), split, split, split, down_split, split, down_split,
                  P(None, "rank"), P("rank", None), vector, vector, vector, vector, P("batch", None)),
        out_specs=(P("batch", None), P("batch", None), vector, vector, vector, vector),
        check_vma=False,
    )
```

```python
import functools
import heapq
import math

import jax
import jax.numpy as jnp
from jax import lax
from jax.experimental import pallas as pl
from jax.experimental.pallas import tpu as pltpu
from jax.sharding import PartitionSpec as P

HEAD_DIM = 64
MESH = pl.DeviceIdType.MESH

epsilon = 1e-05
masked = -1e30

low, f32 = jnp.bfloat16, jnp.float32


def flip(index, bit):
    step = 1 << bit
    return index + step - 2 * step * ((index // step) % 2)


class Exchange:
    LINK, CORE_LINK, LATENCY, CORE_LATENCY, START, WAIT = 45e3, 300e3, 2.6, 1.5, 0.08, 0.03
    LOAD, ENTRY, WINDOW, MARGIN, EARLY = 1.5e6, 8.0, 250e3, 0.2, 1
    AHEAD = 3

    def __init__(self, groups, loads, sems):
        self.groups, self.loads = groups, loads
        self.sems = {link: sems[2 * i : 2 * i + 2] for i, link in enumerate("yxzc")}
        self.batch = lax.axis_index("batch")
        self.rank = lax.axis_index("rank")
        b = self.batch
        self.core = b % 2
        bit_x, bit_z = (b // 2) % 2, (b // 4) % 2
        self.partner = {
            "y": (b, 1 - self.rank),
            "x": (flip(b, 1), self.rank),
            "z": (flip(b, 2), self.rank),
            "c": (flip(b, 0), self.rank),
        }
        chip = lambda cx, cz: cx + 2 * cz
        own, across, along, far = (
            chip(bit_x, bit_z),
            chip(1 - bit_x, bit_z),
            chip(bit_x, 1 - bit_z),
            chip(1 - bit_x, 1 - bit_z),
        )
        parity = (bit_x + bit_z) % 2
        first = lambda who: 2 * who
        second = lambda who: 2 * who + 1
        pair = lambda par, which: 8 + 2 * par + which
        self.y_units = [first(own), second(own), pair(parity, 0), pair(parity, 1)]
        self.x_units = [first(across), second(across), pair(1 - parity, 0), second(far)]
        self.z_units = [first(along), second(along), first(far), pair(1 - parity, 1)]
        self.x_out = [first(own), second(own), pair(parity, 0), second(along)]
        self.z_out = [first(own), second(own), first(across), pair(parity, 1)]
        self.count = 4 * len(groups)
        self.next_tick = 0
        self.here = set()

    def barrier(self):
        bar = pltpu.get_barrier_semaphore()
        for who in self.partner.values():
            pl.semaphore_signal(bar, inc=1, device_id=who, device_id_type=MESH)
        pl.semaphore_wait(bar, len(self.partner))

    def copy(self, src, dst, send, recv, link):
        return pltpu.make_async_remote_copy(
            src_ref=src, dst_ref=dst, send_sem=send, recv_sem=recv,
            device_id=self.partner[link], device_id_type=MESH,
        )

    def move(self, link, item, unit, core, rank):
        ref = self.groups[item // 4].piece(2 * unit + core, rank)
        send, recv = self.sems[link]
        return self.copy(ref, ref, send.at[item // 4], recv.at[item], link)

    def share(self, group, unit, core, rank):
        ref = self.groups[group].piece(2 * unit + core, rank)
        send, recv = self.sems["c"]
        return self.copy(ref, ref, send.at[group], recv.at[group], "c")

    def begin(self, link, item):
        units = {"y": self.y_units, "x": self.x_out, "z": self.z_out}[link]
        self.move(link, item, units[item % 4], self.core, self.rank if link == "y" else 1 - self.rank).start()

    def arrive(self, link, item):
        units = {"y": self.y_units, "x": self.x_units, "z": self.z_units}[link]
        unit = units[item % 4]
        self.move(link, item, unit, self.core, 1 - self.rank).wait_recv()
        self.share(item // 4, unit, self.core, 1 - self.rank).start()

    def sent(self, link, group):
        ref = self.groups[group].many(12 if link == "c" else 4)
        send, recv = self.sems[link]
        self.copy(ref, ref, send.at[group], recv.at[group], link).wait_send()

    def shared(self, group):
        ref = self.groups[group].many(12)
        send, recv = self.sems["c"]
        self.copy(ref, ref, send.at[group], recv.at[group], "c").wait_recv()

    def plan(self, steps):
        size = [group.bytes for group in self.groups]
        now = self.ENTRY
        loaded, at = [], self.ENTRY - 4.0
        for bytes_ in size:
            at += 24 * bytes_ / self.LOAD
            loaded.append(at)
        queue = []
        for group in range(len(size) + self.EARLY):
            if group < len(size):
                queue += [4 * group, 4 * group + 1]
            if group >= self.EARLY:
                queue += [4 * (group - self.EARLY) + 2, 4 * (group - self.EARLY) + 3]
        free = dict.fromkeys("yxzc", 0.0)
        pending, arrived, here, batches, batch = [], {}, {}, [], []

        def send(link, item):
            nonlocal now
            now += self.START
            rate, latency = (self.CORE_LINK, self.CORE_LATENCY) if link == "c" else (self.LINK, self.LATENCY)
            free[link] = max(now, free[link]) + size[item // 4] / rate
            heapq.heappush(pending, (free[link] + latency, len(batches), len(batch), link, item))
            if link != "c":
                batch.append(("begin", link, item))

        def supply():
            while queue:
                item = queue[0]
                behind = max(0.0, free["y"] - now) * self.LINK
                if behind > 1 and behind + size[item // 4] > self.WINDOW or loaded[item // 4] > now:
                    break
                queue.pop(0)
                send("y", item)

        def serve():
            nonlocal now
            supply()
            while pending and pending[0][0] + self.MARGIN <= now:
                *_, link, item = heapq.heappop(pending)
                group, j = divmod(item, 4)
                now += self.WAIT
                if link == "c":
                    here[group] = here.get(group, 0) + 1
                    if here[group] == 12:
                        batch.append(("shared", link, group))
                else:
                    batch.append(("arrive", link, item))
                    if link == "y":
                        for onward in (("x", "z"), ("x", "z"), ("x",), ("z",))[j]:
                            send(onward, item)
                    elif (link, j) == ("x", 0):
                        send("z", 4 * group + 2)
                    elif (link, j) == ("z", 1):
                        send("x", 4 * group + 3)
                    send("c", item)
                supply()

        def pause():
            nonlocal now
            after = [pending[0][0] + self.MARGIN] if pending else []
            if queue:
                item = queue[0]
                room = free["y"] - max(0.0, self.WINDOW - size[item // 4]) / self.LINK
                after.append(max(loaded[item // 4], room))
            now = max(now + 0.02, min(after))

        for length, needed in steps:
            serve()
            while any(here.get(group, 0) < 12 for group in needed):
                pause()
                serve()
            batches.append(batch)
            batch = []
            now += length
        while queue or pending:
            pause()
            serve()
        batches.append(batch)
        self.batches = batches

    def tick(self):
        for kind, link, item in self.batches[self.next_tick]:
            if kind == "begin":
                if link == "y" and item % 4 == 0:
                    for copies in self.loads[item // 4 + self.AHEAD : item // 4 + self.AHEAD + 1]:
                        for copy in copies:
                            copy.start()
                    for copy in self.loads[item // 4]:
                        copy.wait()
                self.begin(link, item)
            elif kind == "arrive":
                self.arrive(link, item)
            else:
                self.shared(item)
                self.here.add(item)
        self.next_tick += 1

    def settle(self):
        for group in range(len(self.groups)):
            for link in "yxzc":
                self.sent(link, group)


class Group:
    def __init__(self, piece, many):
        self.piece, self.many = piece, many
        shape = many(1).shape
        self.bytes = math.prod(shape) * 2


def piece_rows(ref, lead, rows, columns):
    height = rows // 24

    def full(piece, rank):
        start = pl.multiple_of(piece * height, 16)
        left = pl.multiple_of(rank * columns, 128)
        return ref.at[(*lead, pl.ds(start, height), pl.ds(left, columns))]

    return Group(full, lambda n: ref.at[(*lead, pl.ds(0, n * height), pl.ds(0, columns))])


def column_groups(ref, lead, rows, columns, parts):
    height, width = rows // 24, columns // parts

    def group(part):
        def full(piece, rank):
            start = pl.multiple_of(piece * height, 16)
            left = pl.multiple_of(rank * columns + part * width, 128)
            return ref.at[(*lead, pl.ds(start, height), pl.ds(left, width))]

        return Group(full, lambda n: ref.at[(*lead, pl.ds(0, n * height), pl.ds(0, width))])

    return [group(part) for part in range(parts)]


def row_groups(ref, lead, rows, parts):
    height = rows // parts // 24

    def group(part):
        def full(piece, rank):
            start = rank * rows + part * (rows // parts) + piece * height
            return ref.at[(*lead, pl.ds(pl.multiple_of(start, 16), height), slice(None))]

        return Group(full, lambda n: ref.at[(*lead, pl.ds(0, n * height), slice(None))])

    return [group(part) for part in range(parts)]


def tile_group(ref, rows, columns):
    height, width = rows // 8, columns // 3

    def full(piece, rank):
        start = pl.multiple_of(rank * rows + (piece % 8) * height, 16)
        left = pl.multiple_of((piece // 8) * width, 128)
        return ref.at[pl.ds(start, height), pl.ds(left, width)]

    return Group(full, lambda n: ref.at[pl.ds(0, n * height), pl.ds(0, width)])


def dot(left, right):
    return jnp.dot(left, right, preferred_element_type=f32)


def dot_back(left, right):
    return lax.dot_general(left, right, (((1,), (1,)), ((), ())), preferred_element_type=f32)


def dot_turned(left, right):
    return lax.dot_general(left, right, (((0,), (0,)), ((), ())), preferred_element_type=f32)


def normalize(values):
    center = values - jnp.mean(values, axis=-1, keepdims=True)
    spread = jnp.mean(center * center, axis=-1, keepdims=True)
    scale = lax.rsqrt(spread + epsilon)
    return center * scale, scale


def normalize_back(grad, normed, scale):
    shared = jnp.mean(grad * normed, axis=-1, keepdims=True)
    return (grad - jnp.mean(grad, axis=-1, keepdims=True) - normed * shared) * scale


def gelu_and_slope(values):
    cdf = 0.5 + 0.5 * lax.erf(values * 0.5**0.5)
    bell = jnp.exp(-0.5 * values * values) * (2.0 * math.pi) ** -0.5
    return values * cdf, cdf + values * bell


def lane_half(shape, which):
    lanes = lax.broadcasted_iota(jnp.int32, shape, 1)
    return (lanes < HEAD_DIM) if which == 0 else (lanes >= HEAD_DIM)


class Layers:
    def __init__(self, refs):
        self.__dict__.update(refs)
        self.rows, self.model = self.x.shape
        self.heads = self.model // HEAD_DIM
        self.ranks = self.full_a.shape[1]
        self.blocks = [pl.ds(start, 64) for start in range(0, self.rows, 64)]

    def vector(self, name, level):
        return getattr(self, name)[level : level + 1, :]

    def adapt(self, level, tick, need):
        ranks = self.ranks
        tick()
        need("a")
        inner = dot(self.xl[...], self.full_a[...])
        self.inner[...] = inner.astype(low)
        self.hid[:, :ranks] = (inner * self.vector("dq", level)).astype(low)
        self.hid[:, ranks : 2 * ranks] = (inner * self.vector("dv", level)).astype(low)
        tick()
        need("b")
        need("qkv")
        self.att[1] = dot(self.xl[...], self.qkv[level, 1]).astype(low)
        for i, (which, scale) in enumerate(((0, "bq"), (2, "bv"))):
            tick()
            lift = dot(self.hid[:, i * ranks : (i + 1) * ranks], self.full_b[...])
            self.lift[i] = lift.astype(low)
            rows = (dot(self.xl[...], self.qkv[level, which]) + lift * self.vector(scale, level)).astype(low)
            self.att[which] = rows if which else (rows.astype(f32) * HEAD_DIM**-0.5).astype(low)

    def attend(self, tick):
        width = 2 * HEAD_DIM
        bias = self.bias[...]
        bias = jnp.concatenate([bias] * (self.rows // bias.shape[1]), axis=1)
        for pair in range(self.heads // 2):
            tick()
            slab = slice(pair * width, (pair + 1) * width)
            query, keys, values = (self.att[i, :, slab] for i in range(3))
            first = lane_half(query.shape, 0)
            mixed = []
            for which in range(2):
                chosen = jnp.where(first == (which == 0), query, jnp.zeros_like(query))
                scores = dot_back(keys, chosen) + bias
                peak = jnp.max(scores, axis=0, keepdims=True)
                exponent = jnp.exp(scores - peak)
                total = jnp.sum(exponent, axis=0, keepdims=True)
                probs = (exponent * (1.0 / total)).astype(low)
                self.probs[2 * pair + which] = probs
                mixed.append(dot_turned(probs, values))
            self.mix[:, slab] = jnp.where(first, *mixed).astype(low)

    def project(self, level, tick, need):
        tick()
        need("out")
        self.f2[...] = self.x[...] + dot(self.mix[...], self.out[level])
        for part in self.blocks:
            normed, scale = normalize(self.f2[part, :])
            self.f2[part, :] = normed
            self.normed[2 * level, part, :] = normed.astype(low)
            self.scale[2 * level, part, :] = scale

    def feed(self, level, rank, tick, need):
        hidden = self.hid.shape[1]
        width = hidden // 6
        for chunk in range(6):
            tick()
            if chunk == 3:
                need("up")
            columns = pl.ds(pl.multiple_of((rank * 3 + chunk) % 6 * width, 128), width)
            before = dot(self.normed[2 * level], self.up[level, :, columns])
            active, slope = gelu_and_slope(before)
            self.hid[:, columns] = active.astype(low)
            self.slope[:, columns] = slope.astype(low)
        half = hidden // 2
        for start, group in ((0, None), (half, "down")):
            tick()
            if group:
                need(group)
            units = pl.ds(pl.multiple_of((rank * half + start) % hidden, 128), half)
            self.f2[...] += dot(self.hid[:, units], self.down[level, units, :])
        for part in self.blocks:
            normed, scale = normalize(self.f2[part, :])
            self.x[part, :] = normed
            self.xl[part, :] = normed.astype(low)
            self.normed[2 * level + 1, part, :] = normed.astype(low)
            self.scale[2 * level + 1, part, :] = scale


    def norm_back(self, index, src):
        for part in self.blocks:
            grad = normalize_back(src[part, :].astype(f32), self.normed[index, part, :].astype(f32), self.scale[index, part, :])
            self.f2[part, :] = grad
            self.xl[part, :] = grad.astype(low)

    def feed_back(self, level, grad, tick):
        self.norm_back(2 * level + 1, grad)
        hidden = self.hid.shape[1]
        width = hidden // 6
        for chunk in range(6):
            columns = slice(chunk * width, (chunk + 1) * width)
            grad = dot_back(self.xl[...], self.down[level, columns, :])
            self.hid[:, columns] = (grad * self.slope[:, columns].astype(f32)).astype(low)
            if chunk % 3 == 2:
                tick()
        self.f2[...] += dot_back(self.hid[...], self.up[level])
        tick()
        self.norm_back(2 * level, self.f2)
        self.mix[...] = dot_back(self.xl[...], self.out[level]).astype(low)
        tick()

    def attend_back(self, tick):
        width = 2 * HEAD_DIM
        for pair in range(self.heads // 2):
            slab = slice(pair * width, (pair + 1) * width)
            query, keys, values = (self.att[i, :, slab] for i in range(3))
            grad = self.mix[:, slab]
            first = lane_half(values.shape, 0)
            grads = [], [], []
            for which in range(2):
                probs = self.probs[2 * pair + which]
                chosen = jnp.where(first == (which == 0), values, jnp.zeros_like(values))
                wide = probs.astype(f32)
                shared = wide * dot_back(chosen, grad)
                delta = jnp.sum(shared, axis=0, keepdims=True)
                dscore = (shared - wide * delta).astype(low)
                grads[0].append(dot_turned(dscore, keys))
                grads[1].append(dot(dscore, query))
                grads[2].append(dot(probs, grad))
            self.att[0, :, slab] = (jnp.where(first, *grads[0]) * HEAD_DIM**-0.5).astype(low)
            self.att[1, :, slab] = jnp.where(first, *grads[1]).astype(low)
            self.att[2, :, slab] = jnp.where(first, *grads[2]).astype(low)
            tick()

    def vectors_back(self, level, part):
        ranks = self.ranks
        total = lambda grid: jnp.sum(grid, axis=0, keepdims=True)
        sums, passed = {}, {}
        for i, (which, scale, name) in enumerate(((0, "bq", "q"), (2, "bv", "v"))):
            rows = self.att[which, part, :].astype(f32)
            sums["b" + name] = total(rows * self.lift[i, part, :].astype(f32))
            passed[name] = slice((1 + i) * ranks, (1 + i) * ranks + self.model)
            self.hid[part, passed[name]] = (rows * self.vector(scale, level)).astype(low)
        found = {"dq": [], "dv": []}
        for columns in (slice(0, ranks // 2), slice(ranks // 2, ranks)):
            inner = self.inner[part, columns].astype(f32)
            grad = 0.0
            for name in ("q", "v"):
                back = dot_back(self.hid[part, passed[name]], self.full_b[columns, :])
                found["d" + name].append(total(back * inner))
                grad += back * self.vector("d" + name, level)[:, columns]
            self.hid[part, columns] = grad.astype(low)
        sums.update({name: jnp.concatenate(pieces, axis=1) for name, pieces in found.items()})
        return sums

    def input_back(self, level, part):
        grad = self.f2[part, :] + dot_back(self.hid[part, : self.ranks], self.full_a[...])
        for i in range(3):
            grad += dot_back(self.att[i, part, :], self.qkv[level, i])
        self.x[part, :] = grad


def layers_kernel(levels, names, groups_of, *refs):
    refs = dict(zip(names, refs))
    get = refs.pop
    ins = [get(n) for n in INPUTS]
    (tokens, lengths, wq, wk, wv, wo, wu, wd, mat_a, mat_b, dq, bq, dv, bv, cotangent) = ins
    rank, batch = lax.axis_index("rank"), lax.axis_index("batch")
    both = refs["x"].shape[0]
    seq = both
    model, feat = wq.shape[1:]
    hidden, rank_part = wu.shape[2], mat_a.shape[1]
    own_x, other_x, own_g, other_g, out_sums = (get(n) for n in ("own_x", "other_x", "own_g", "other_g", "out_sums"))
    spills = [get("spill_probs"), get("spill_att"), get("spill_lift"), get("spill_inner"), get("spill_slope")]
    load_sem, spill_sem, small_send, small_recv = (get(n) for n in ("load_sem", "spill_sem", "small_send", "small_recv"))
    sems = [get(f"sem{i}") for i in range(8)]
    swap_send, swap_recv, sum_send, sum_recv = (get(n) for n in ("swap_send", "swap_recv", "sum_send", "sum_recv"))
    store_sem = get("store_sem")
    gone, came = get("gone"), get("came")
    sum_buf, sum_in, sums_ref = get("sum_buf"), get("sum_in"), get("sums")
    layers = Layers(refs)
    L = layers

    used = [0]

    def load(src, dst):
        copy = pltpu.make_async_copy(src, dst, load_sem.at[used[0]])
        used[0] += 1
        return copy

    def columns_of(size):
        return pl.ds(pl.multiple_of(rank * size, 128), size)

    def rows_of(size):
        return pl.ds(pl.multiple_of(rank * size, 16), size)

    own_rows = rows_of(seq)

    groups, loads, names_of = [], [], {}

    def add(name, found, copies):
        for i, group in enumerate(found):
            names_of[name + (str(i) if len(found) > 1 else "")] = len(groups)
            groups.append(group)
            loads.append(copies if i == 0 else [])

    add("a", [piece_rows(L.full_a, (), model, rank_part)], [load(mat_a, L.full_a.at[:, columns_of(rank_part)])])
    load_x = load(tokens.at[own_rows, :], L.xl)
    add("b", [tile_group(L.full_b, rank_part, model)], [load(mat_b, L.full_b.at[rows_of(rank_part), :])])
    for level in range(levels):
        add(f"qkv/{level}", [piece_rows(L.qkv, (level, slice(None)), model, feat)], [
            load(w.at[level], L.qkv.at[level, i, :, columns_of(feat)]) for i, w in enumerate((wq, wk, wv))])
        add(f"out/{level}", row_groups(L.out, (level,), feat, 1), [
            load(wo.at[level], L.out.at[level, rows_of(feat), :])])
        add(f"up/{level}", column_groups(L.up, (level,), model, hidden, 1), [
            load(wu.at[level], L.up.at[level, :, columns_of(hidden)])])
        add(f"down/{level}", row_groups(L.down, (level,), hidden, 1), [
            load(wd.at[level], L.down.at[level, rows_of(hidden), :])])
    vectors = [(dq, L.dq), (bq, L.bq), (dv, L.dv), (bv, L.bv)]

    small_loads = [load(src, dst.at[:, columns_of(src.shape[1])]) for src, dst in vectors]
    load_g = load(cotangent.at[own_rows, :], gone)
    exchange = Exchange(groups, loads, sems)
    for copies in (small_loads, *loads[: exchange.AHEAD], [load_x]):
        for copy in copies:
            copy.start()
    bits = (lax.axis_size("batch") - 1).bit_length()
    for bit in range(3, bits):
        exchange.partner[bit] = (flip(batch, bit), rank)
    exchange.barrier()
    small = []
    for i, (src, dst) in enumerate(vectors):
        ref = dst.at[:, columns_of(src.shape[1])]
        small_loads[i].wait()
        small.append(exchange.copy(ref, ref, small_send.at[i], small_recv.at[i], "y"))
        small[-1].start()

    slots = lax.broadcasted_iota(jnp.int32, L.bias.shape, 0)
    length = lengths[rank]
    L.bias[...] = jnp.where(slots < length, 0.0, masked)

    steps = []
    for level in range(levels):
        at = lambda name: [names_of[f"{name}/{level}"]]
        steps += [(1.3, [names_of["a"]]), (0.75, [names_of["b"]] + at("qkv")), (1.2, []), (1.2, [])]
        steps += [(0.86, [])] * (L.heads // 2) + [(1.0, at("out"))]
        steps += [(0.42, at("up") if chunk == 3 else []) for chunk in range(6)]
        steps += [(1.3, []), (1.8, at("down"))]
    exchange.plan(steps)
    load_x.wait()

    L.x[...] = L.xl[...].astype(f32)
    for copy in small:
        copy.wait()

    spill_src = [L.probs, L.att, L.lift, L.inner, L.slope]
    spill = [pltpu.make_async_copy(src, dst, spill_sem.at[i]) for i, (src, dst) in enumerate(zip(spill_src, spills))]
    fetch = [pltpu.make_async_copy(dst, src, spill_sem.at[i]) for i, (src, dst) in enumerate(zip(spill_src, spills))]
    PROBS, ATT, LIFT, INNER, SLOPE = range(5)

    for level in range(levels):
        def need(name):
            assert names_of[name if name in "ab" else f"{name}/{level}"] in exchange.here

        if level:
            for i in (ATT, LIFT, INNER, PROBS):
                spill[i].wait()
        L.adapt(level, exchange.tick, need)
        if not level:
            spill[LIFT].start()
            spill[INNER].start()
        L.attend(exchange.tick)
        if not level:
            spill[ATT].start()
            spill[PROBS].start()
        L.project(level, exchange.tick, need)
        if level:
            spill[SLOPE].wait()
        L.feed(level, rank, exchange.tick, need)
        if not level:
            spill[SLOPE].start()
    exchange.tick()
    load_g.start()

    def swap(src, index, part, slot):
        return exchange.copy(src.at[part, :], came.at[index, part], swap_send.at[index + slot],
                             swap_recv.at[index + slot], "y")

    first_rows = seq // 4
    store_own = pltpu.make_async_copy(L.x, own_x, store_sem.at[0])
    store_own.start()
    swaps = [swap(L.normed.at[2 * levels - 1], 0, pl.ds(0, seq), 0)]
    swaps[0].start()
    load_g.wait()

    def sum_copy(level, step):
        who = ["y", "c", "x", "z", *range(3, bits)][step]
        src = sum_buf.at[level, 1 - rank] if step == 0 else sum_buf.at[level, rank]
        return exchange.copy(src, sum_in.at[level, step], sum_send.at[level, step], sum_recv.at[level, step], who)

    def sum_step(level, step):
        if step:
            sum_copy(level, step - 1).wait()
            sum_buf[level, rank] += sum_in[level, step - 1]
        if step < 1 + bits:
            sum_copy(level, step).start()

    later = []

    def step_on():
        if later:
            later.pop(0)()

    ORDER = (("dq", rank_part), ("bq", feat), ("dv", rank_part), ("bv", feat))
    for level in reversed(range(levels)):
        last = level == 0
        L.feed_back(level, L.x if level < levels - 1 else gone, step_on)
        if not last:
            fetch[SLOPE].start()
        elif levels > 1:
            fetch[ATT].wait()
            fetch[PROBS].wait()
        L.attend_back(step_on)
        if not last:
            fetch[PROBS].start()
        elif levels > 1:
            fetch[LIFT].wait()
            fetch[INNER].wait()
        if level == levels - 1:
            store_own.wait()
        sums = [{}]
        parts = [pl.ds(0, seq)]
        if last:
            parts = [pl.ds(0, first_rows), pl.ds(first_rows, seq - first_rows)]
        for i, part in enumerate(parts):
            found = L.vectors_back(level, part)
            sums = {name: found[name] + sums[name] if i else found[name] for name in found}
            if i == len(parts) - 1:
                at = 0
                for name, width in ORDER:
                    for side in range(2):
                        sum_buf[level, side, :, pl.ds(at, width)] = sums[name][:, side * width : (side + 1) * width]
                    at += width
                while later:
                    step_on()
                for step in range(2 + bits):
                    later.append(functools.partial(sum_step, level, step))
                step_on()
            L.input_back(level, part)
            if last:
                gone[part, :] = L.x[part, :].astype(low)
                swaps.append(swap(gone, 1, part, i))
                swaps[-1].start()
        if not last:
            for i in (ATT, LIFT, INNER):
                fetch[i].start()
            fetch[SLOPE].wait()
    store_g = pltpu.make_async_copy(L.x, own_g, store_sem.at[1])
    store_g.start()
    exchange.settle()
    swaps[0].wait()
    store_came = [pltpu.make_async_copy(came.at[0], other_x, store_sem.at[2])]
    store_came[0].start()
    while later:
        step_on()
    for level in range(levels):
        sums_ref[level : level + 1, :] = sum_buf[level, rank]
    store_sums = pltpu.make_async_copy(sums_ref, out_sums, store_sem.at[5])
    store_sums.start()
    for i, part in enumerate(parts):
        swaps[1 + i].wait()
        store_came.append(pltpu.make_async_copy(came.at[1, part], other_g.at[part, :], store_sem.at[3 + i]))
        store_came[-1].start()
    store_g.wait()
    store_sums.wait()
    for copy in store_came:
        copy.wait()


def assemble_kernel(rank_part, feat, own_x, other_x, own_g, other_g, sums, out_x, out_g, *refs):
    out_vectors, (own, came, wide, vectors, load_sem, store_sem) = refs[:4], refs[4:]
    rank = lax.axis_index("rank")
    seq = own_x.shape[0]
    place = lambda who: pl.ds(pl.multiple_of(who * seq, 16), seq)
    loads = [pltpu.make_async_copy(sums, vectors, load_sem.at[4])]
    for i, (mine, other) in enumerate(((own_x, other_x), (own_g, other_g))):
        loads.append(pltpu.make_async_copy(other, came.at[i], load_sem.at[2 * i]))
        loads.append(pltpu.make_async_copy(mine, own.at[i], load_sem.at[2 * i + 1]))
    for copy in loads:
        copy.start()
    stores = []

    def store(src, dst):
        stores.append(pltpu.make_async_copy(src, dst, store_sem.at[len(stores)]))
        stores[-1].start()

    for i, out in enumerate((out_x, out_g)):
        loads[1 + 2 * i].wait()
        wide[i] = came[i].astype(f32)
        store(wide.at[i], out.at[place(1 - rank), :])
        loads[2 + 2 * i].wait()
        store(own.at[i], out.at[place(rank), :])
    loads[0].wait()
    at = 0
    for width, dst in zip((rank_part, feat, rank_part, feat), out_vectors):
        store(vectors.at[:, pl.ds(at, width)], dst)
        at += width
    for copy in stores:
        copy.wait()


INPUTS = ("tokens", "lengths", "wq", "wk", "wv", "wo", "wu", "wd", "mat_a", "mat_b",
          "s_dq", "s_bq", "s_dv", "s_bv", "cotangent")


def on_device(tokens, valid_len, w_query, w_key, w_value, w_out, w_up, w_down, mat_a, mat_b,
              scale_dq, scale_bq, scale_dv, scale_bv, cotangent):
    levels, model, feat = w_query.shape
    hidden, rank_part = w_up.shape[2], mat_a.shape[1]
    ranks = 2
    rows = tokens.shape[0]
    seq = rows // valid_len.shape[0]
    heads = ranks * feat // HEAD_DIM
    bits = (lax.axis_size("batch") - 1).bit_length()
    count = 4 * (2 + 4 * levels)
    shape = jax.ShapeDtypeStruct
    dma = lambda *n: pltpu.SemaphoreType.DMA(n)
    any_spec = pl.BlockSpec(memory_space=pl.ANY)
    smem_spec = pl.BlockSpec(memory_space=pltpu.SMEM)
    vmem = pltpu.VMEM
    sum_width = 2 * (rank_part + feat)
    outs = dict(
        own_x=shape((seq, model), f32),
        other_x=shape((seq, model), low),
        own_g=shape((seq, model), f32),
        other_g=shape((seq, model), low),
        out_sums=shape((levels, sum_width), f32),
        spill_probs=shape((heads, seq, seq), low),
        spill_att=shape((3, seq, model), low),
        spill_lift=shape((2, seq, model), low),
        spill_inner=shape((seq, ranks * rank_part), low),
        spill_slope=shape((seq, ranks * hidden), low),
    )
    scratch = dict(
        qkv=vmem((levels, 3, model, ranks * feat), low),
        out=vmem((levels, ranks * feat, model), low),
        up=vmem((levels, model, ranks * hidden), low),
        down=vmem((levels, ranks * hidden, model), low),
        full_a=vmem((model, ranks * rank_part), low),
        full_b=vmem((ranks * rank_part, model), low),
        dq=vmem((levels, ranks * rank_part), f32),
        bq=vmem((levels, ranks * feat), f32),
        dv=vmem((levels, ranks * rank_part), f32),
        bv=vmem((levels, ranks * feat), f32),
        bias=vmem((seq, 128), f32),
        x=vmem((seq, model), f32),
        xl=vmem((seq, model), low),
        f2=vmem((seq, model), f32),
        hid=vmem((seq, ranks * hidden), low),
        att=vmem((3, seq, model), low),
        lift=vmem((2, seq, model), low),
        inner=vmem((seq, ranks * rank_part), low),
        probs=vmem((heads, seq, seq), low),
        mix=vmem((seq, model), low),
        normed=vmem((2 * levels, seq, model), low),
        scale=vmem((2 * levels, seq, 1), f32),
        slope=vmem((seq, ranks * hidden), low),
        gone=vmem((seq, model), low),
        came=vmem((2, seq, model), low),
        sum_buf=vmem((levels, 2, 1, sum_width), f32),
        sum_in=vmem((levels, 1 + bits, 1, sum_width), f32),
        load_sem=dma(4 + 6 * levels + 6),
        spill_sem=dma(5),
        small_send=dma(4),
        small_recv=dma(4),
        swap_send=dma(4),
        swap_recv=dma(4),
        sum_send=dma(levels, 1 + bits),
        sum_recv=dma(levels, 1 + bits),
        store_sem=dma(6),
        sums=vmem((levels, sum_width), f32),
    )
    for i in range(8):
        scratch[f"sem{i}"] = dma(count if i in (1, 3, 5) else count // 4)
    names = INPUTS + tuple(outs) + tuple(scratch)
    vectors = (scale_dq, scale_bq, scale_dv, scale_bv)
    macs = seq * model * (5 * ranks * rank_part + 8 * ranks * feat + 4 * ranks * hidden) * levels
    results = pl.pallas_call(
        functools.partial(layers_kernel, levels, names, None),
        out_shape=tuple(outs.values()),
        in_specs=[any_spec, smem_spec] + [any_spec] * 13,
        out_specs=(any_spec,) * 10,
        scratch_shapes=list(scratch.values()),
        compiler_params=pltpu.CompilerParams(
            collective_id=0, has_side_effects=True, vmem_limit_bytes=64 * 2**20 - 2**18),
        cost_estimate=pl.CostEstimate(flops=2 * macs, bytes_accessed=64 * 2**20, transcendentals=0),
        name="layers",
    )(tokens, valid_len, w_query, w_key, w_value, w_out, w_up, w_down, mat_a, mat_b, *vectors, cotangent)
    return pl.pallas_call(
        functools.partial(assemble_kernel, rank_part, feat),
        out_shape=(shape((rows, model), f32),) * 2
        + tuple(shape((levels, width), f32) for width in (rank_part, feat, rank_part, feat)),
        in_specs=[pl.BlockSpec(memory_space=pltpu.HBM)] * 5,
        out_specs=(any_spec,) * 6,
        scratch_shapes=[vmem((2, seq, model), f32), vmem((2, seq, model), low), vmem((2, seq, model), f32),
                        vmem((levels, sum_width), f32), dma(5), dma(8)],
        compiler_params=pltpu.CompilerParams(vmem_limit_bytes=63 * 2**20),
        name="assemble",
    )(*results[:5])


def solution(mesh):
    split = P(None, None, "rank")
    down_split = P(None, "rank", None)
    vector = P(None, "rank")
    return jax.shard_map(
        on_device,
        mesh=mesh,
        in_specs=(P("batch", None), P("batch"), split, split, split, down_split, split, down_split,
                  P(None, "rank"), P("rank", None), vector, vector, vector, vector, P("batch", None)),
        out_specs=(P("batch", None), P("batch", None), vector, vector, vector, vector),
        check_vma=False,
    )
```

```python
import functools
import heapq
import math

import jax
import jax.numpy as jnp
from jax import lax
from jax.experimental import pallas as pl
from jax.experimental.pallas import tpu as pltpu
from jax.sharding import PartitionSpec as P

HEAD_DIM = 64
MESH = pl.DeviceIdType.MESH

epsilon = 1e-05
masked = -1e30

low, f32 = jnp.bfloat16, jnp.float32


def flip(index, bit):
    step = 1 << bit
    return index + step - 2 * step * ((index // step) % 2)


class Exchange:
    LINK, CORE_LINK, LATENCY, CORE_LATENCY, START, WAIT = 45e3, 300e3, 2.6, 1.5, 0.08, 0.03
    LOAD, ENTRY, WINDOW, MARGIN, EARLY = 1.5e6, 8.0, 250e3, 0.2, 1
    AHEAD = 3

    def __init__(self, groups, loads, sems):
        self.groups, self.loads = groups, loads
        self.sems = {link: sems[2 * i : 2 * i + 2] for i, link in enumerate("yxzc")}
        self.batch = lax.axis_index("batch")
        self.rank = lax.axis_index("rank")
        b = self.batch
        self.core = b % 2
        bit_x, bit_z = (b // 2) % 2, (b // 4) % 2
        self.partner = {
            "y": (b, 1 - self.rank),
            "x": (flip(b, 1), self.rank),
            "z": (flip(b, 2), self.rank),
            "c": (flip(b, 0), self.rank),
        }
        chip = lambda cx, cz: cx + 2 * cz
        own, across, along, far = (
            chip(bit_x, bit_z),
            chip(1 - bit_x, bit_z),
            chip(bit_x, 1 - bit_z),
            chip(1 - bit_x, 1 - bit_z),
        )
        parity = (bit_x + bit_z) % 2
        first = lambda who: 2 * who
        second = lambda who: 2 * who + 1
        pair = lambda par, which: 8 + 2 * par + which
        self.y_units = [first(own), second(own), pair(parity, 0), pair(parity, 1)]
        self.x_units = [first(across), second(across), pair(1 - parity, 0), second(far)]
        self.z_units = [first(along), second(along), first(far), pair(1 - parity, 1)]
        self.x_out = [first(own), second(own), pair(parity, 0), second(along)]
        self.z_out = [first(own), second(own), first(across), pair(parity, 1)]
        self.count = 4 * len(groups)
        self.next_tick = 0
        self.here = set()

    def barrier(self):
        bar = pltpu.get_barrier_semaphore()
        for who in self.partner.values():
            pl.semaphore_signal(bar, inc=1, device_id=who, device_id_type=MESH)
        pl.semaphore_wait(bar, len(self.partner))

    def copy(self, src, dst, send, recv, link):
        return pltpu.make_async_remote_copy(
            src_ref=src, dst_ref=dst, send_sem=send, recv_sem=recv,
            device_id=self.partner[link], device_id_type=MESH,
        )

    def move(self, link, item, unit, core, rank):
        ref = self.groups[item // 4].piece(2 * unit + core, rank)
        send, recv = self.sems[link]
        return self.copy(ref, ref, send.at[item // 4], recv.at[item], link)

    def share(self, group, unit, core, rank):
        ref = self.groups[group].piece(2 * unit + core, rank)
        send, recv = self.sems["c"]
        return self.copy(ref, ref, send.at[group], recv.at[group], "c")

    def begin(self, link, item):
        units = {"y": self.y_units, "x": self.x_out, "z": self.z_out}[link]
        self.move(link, item, units[item % 4], self.core, self.rank if link == "y" else 1 - self.rank).start()

    def arrive(self, link, item):
        units = {"y": self.y_units, "x": self.x_units, "z": self.z_units}[link]
        unit = units[item % 4]
        self.move(link, item, unit, self.core, 1 - self.rank).wait_recv()
        self.share(item // 4, unit, self.core, 1 - self.rank).start()

    def sent(self, link, group):
        ref = self.groups[group].many(12 if link == "c" else 4)
        send, recv = self.sems[link]
        self.copy(ref, ref, send.at[group], recv.at[group], link).wait_send()

    def shared(self, group):
        ref = self.groups[group].many(12)
        send, recv = self.sems["c"]
        self.copy(ref, ref, send.at[group], recv.at[group], "c").wait_recv()

    def plan(self, steps):
        size = [group.bytes for group in self.groups]
        now = self.ENTRY
        loaded, at = [], self.ENTRY - 4.0
        for bytes_ in size:
            at += 24 * bytes_ / self.LOAD
            loaded.append(at)
        queue = []
        for group in range(len(size) + self.EARLY):
            if group < len(size):
                queue += [4 * group, 4 * group + 1]
            if group >= self.EARLY:
                queue += [4 * (group - self.EARLY) + 2, 4 * (group - self.EARLY) + 3]
        free = dict.fromkeys("yxzc", 0.0)
        pending, arrived, here, batches, batch = [], {}, {}, [], []

        def send(link, item):
            nonlocal now
            now += self.START
            rate, latency = (self.CORE_LINK, self.CORE_LATENCY) if link == "c" else (self.LINK, self.LATENCY)
            free[link] = max(now, free[link]) + size[item // 4] / rate
            heapq.heappush(pending, (free[link] + latency, len(batches), len(batch), link, item))
            if link != "c":
                batch.append(("begin", link, item))

        def supply():
            while queue:
                item = queue[0]
                behind = max(0.0, free["y"] - now) * self.LINK
                if behind > 1 and behind + size[item // 4] > self.WINDOW or loaded[item // 4] > now:
                    break
                queue.pop(0)
                send("y", item)

        def serve():
            nonlocal now
            supply()
            while pending and pending[0][0] + self.MARGIN <= now:
                *_, link, item = heapq.heappop(pending)
                group, j = divmod(item, 4)
                now += self.WAIT
                if link == "c":
                    here[group] = here.get(group, 0) + 1
                    if here[group] == 12:
                        batch.append(("shared", link, group))
                else:
                    batch.append(("arrive", link, item))
                    if link == "y":
                        for onward in (("x", "z"), ("x", "z"), ("x",), ("z",))[j]:
                            send(onward, item)
                    elif (link, j) == ("x", 0):
                        send("z", 4 * group + 2)
                    elif (link, j) == ("z", 1):
                        send("x", 4 * group + 3)
                    send("c", item)
                supply()

        def pause():
            nonlocal now
            after = [pending[0][0] + self.MARGIN] if pending else []
            if queue:
                item = queue[0]
                room = free["y"] - max(0.0, self.WINDOW - size[item // 4]) / self.LINK
                after.append(max(loaded[item // 4], room))
            now = max(now + 0.02, min(after))

        for length, needed in steps:
            serve()
            while any(here.get(group, 0) < 12 for group in needed):
                pause()
                serve()
            batches.append(batch)
            batch = []
            now += length
        while queue or pending:
            pause()
            serve()
        batches.append(batch)
        self.batches = batches

    def tick(self):
        for kind, link, item in self.batches[self.next_tick]:
            if kind == "begin":
                if link == "y" and item % 4 == 0:
                    for copies in self.loads[item // 4 + self.AHEAD : item // 4 + self.AHEAD + 1]:
                        for copy in copies:
                            copy.start()
                    for copy in self.loads[item // 4]:
                        copy.wait()
                self.begin(link, item)
            elif kind == "arrive":
                self.arrive(link, item)
            else:
                self.shared(item)
                self.here.add(item)
        self.next_tick += 1

    def settle(self):
        for group in range(len(self.groups)):
            for link in "yxzc":
                self.sent(link, group)


class Group:
    def __init__(self, piece, many):
        self.piece, self.many = piece, many
        shape = many(1).shape
        self.bytes = math.prod(shape) * 2


def piece_rows(ref, lead, rows, columns):
    height = rows // 24

    def full(piece, rank):
        start = pl.multiple_of(piece * height, 16)
        left = pl.multiple_of(rank * columns, 128)
        return ref.at[(*lead, pl.ds(start, height), pl.ds(left, columns))]

    return Group(full, lambda n: ref.at[(*lead, pl.ds(0, n * height), pl.ds(0, columns))])


def column_groups(ref, lead, rows, columns, parts):
    height, width = rows // 24, columns // parts

    def group(part):
        def full(piece, rank):
            start = pl.multiple_of(piece * height, 16)
            left = pl.multiple_of(rank * columns + part * width, 128)
            return ref.at[(*lead, pl.ds(start, height), pl.ds(left, width))]

        return Group(full, lambda n: ref.at[(*lead, pl.ds(0, n * height), pl.ds(0, width))])

    return [group(part) for part in range(parts)]


def row_groups(ref, lead, rows, parts):
    height = rows // parts // 24

    def group(part):
        def full(piece, rank):
            start = rank * rows + part * (rows // parts) + piece * height
            return ref.at[(*lead, pl.ds(pl.multiple_of(start, 16), height), slice(None))]

        return Group(full, lambda n: ref.at[(*lead, pl.ds(0, n * height), slice(None))])

    return [group(part) for part in range(parts)]


def tile_group(ref, rows, columns):
    height, width = rows // 8, columns // 3

    def full(piece, rank):
        start = pl.multiple_of(rank * rows + (piece % 8) * height, 16)
        left = pl.multiple_of((piece // 8) * width, 128)
        return ref.at[pl.ds(start, height), pl.ds(left, width)]

    return Group(full, lambda n: ref.at[pl.ds(0, n * height), pl.ds(0, width)])


def dot(left, right):
    return jnp.dot(left, right, preferred_element_type=f32)


def dot_back(left, right):
    return lax.dot_general(left, right, (((1,), (1,)), ((), ())), preferred_element_type=f32)


def dot_turned(left, right):
    return lax.dot_general(left, right, (((0,), (0,)), ((), ())), preferred_element_type=f32)


def normalize(values):
    center = values - jnp.mean(values, axis=-1, keepdims=True)
    spread = jnp.mean(center * center, axis=-1, keepdims=True)
    scale = lax.rsqrt(spread + epsilon)
    return center * scale, scale


def normalize_back(grad, normed, scale):
    shared = jnp.mean(grad * normed, axis=-1, keepdims=True)
    return (grad - jnp.mean(grad, axis=-1, keepdims=True) - normed * shared) * scale


def gelu_and_slope(values):
    cdf = 0.5 + 0.5 * lax.erf(values * 0.5**0.5)
    bell = jnp.exp(-0.5 * values * values) * (2.0 * math.pi) ** -0.5
    return values * cdf, cdf + values * bell


def lane_half(shape, which):
    lanes = lax.broadcasted_iota(jnp.int32, shape, 1)
    return (lanes < HEAD_DIM) if which == 0 else (lanes >= HEAD_DIM)


class Layers:
    def __init__(self, refs):
        self.__dict__.update(refs)
        self.rows, self.model = self.x.shape
        self.heads = self.model // HEAD_DIM
        self.ranks = self.full_a.shape[1]
        self.blocks = [pl.ds(start, 64) for start in range(0, self.rows, 64)]

    def vector(self, name, level):
        return getattr(self, name)[level : level + 1, :]

    def adapt(self, level, tick, need):
        ranks = self.ranks
        tick()
        need("a")
        inner = dot(self.xl[...], self.full_a[...])
        self.inner[...] = inner.astype(low)
        self.hid[:, :ranks] = (inner * self.vector("dq", level)).astype(low)
        self.hid[:, ranks : 2 * ranks] = (inner * self.vector("dv", level)).astype(low)
        tick()
        need("b")
        need("qkv")
        self.att[1] = dot(self.xl[...], self.qkv[level, 1]).astype(low)
        for i, (which, scale) in enumerate(((0, "bq"), (2, "bv"))):
            tick()
            lift = dot(self.hid[:, i * ranks : (i + 1) * ranks], self.full_b[...])
            self.lift[i] = lift.astype(low)
            rows = (dot(self.xl[...], self.qkv[level, which]) + lift * self.vector(scale, level)).astype(low)
            self.att[which] = rows if which else (rows.astype(f32) * HEAD_DIM**-0.5).astype(low)

    def attend(self, tick):
        width = 2 * HEAD_DIM
        bias = self.bias[...]
        bias = jnp.concatenate([bias] * (self.rows // bias.shape[1]), axis=1)
        for pair in range(self.heads // 2):
            tick()
            slab = slice(pair * width, (pair + 1) * width)
            query, keys, values = (self.att[i, :, slab] for i in range(3))
            first = lane_half(query.shape, 0)
            mixed = []
            for which in range(2):
                chosen = jnp.where(first == (which == 0), query, jnp.zeros_like(query))
                scores = dot_back(keys, chosen) + bias
                peak = jnp.max(scores, axis=0, keepdims=True)
                exponent = jnp.exp(scores - peak)
                total = jnp.sum(exponent, axis=0, keepdims=True)
                probs = (exponent * (1.0 / total)).astype(low)
                self.probs[2 * pair + which] = probs
                mixed.append(dot_turned(probs, values))
            self.mix[:, slab] = jnp.where(first, *mixed).astype(low)

    def project(self, level, tick, need):
        tick()
        need("out")
        self.f2[...] = self.x[...] + dot(self.mix[...], self.out[level])
        for part in self.blocks:
            normed, scale = normalize(self.f2[part, :])
            self.f2[part, :] = normed
            self.normed[2 * level, part, :] = normed.astype(low)
            self.scale[2 * level, part, :] = scale

    def feed(self, level, rank, tick, need):
        hidden = self.hid.shape[1]
        width = hidden // 6
        for chunk in range(6):
            tick()
            if chunk == 3:
                need("up")
            columns = pl.ds(pl.multiple_of((rank * 3 + chunk) % 6 * width, 128), width)
            before = dot(self.normed[2 * level], self.up[level, :, columns])
            active, slope = gelu_and_slope(before)
            self.hid[:, columns] = active.astype(low)
            self.slope[:, columns] = slope.astype(low)
        half = hidden // 2
        for start, group in ((0, None), (half, "down")):
            tick()
            if group:
                need(group)
            units = pl.ds(pl.multiple_of((rank * half + start) % hidden, 128), half)
            self.f2[...] += dot(self.hid[:, units], self.down[level, units, :])
        for part in self.blocks:
            normed, scale = normalize(self.f2[part, :])
            self.x[part, :] = normed
            self.xl[part, :] = normed.astype(low)
            self.normed[2 * level + 1, part, :] = normed.astype(low)
            self.scale[2 * level + 1, part, :] = scale


    def norm_back(self, index, src):
        for part in self.blocks:
            grad = normalize_back(src[part, :].astype(f32), self.normed[index, part, :].astype(f32), self.scale[index, part, :])
            self.f2[part, :] = grad
            self.xl[part, :] = grad.astype(low)

    def feed_back(self, level, grad, tick):
        self.norm_back(2 * level + 1, grad)
        hidden = self.hid.shape[1]
        width = hidden // 6
        for chunk in range(6):
            columns = slice(chunk * width, (chunk + 1) * width)
            grad = dot_back(self.xl[...], self.down[level, columns, :])
            self.hid[:, columns] = (grad * self.slope[:, columns].astype(f32)).astype(low)
            if chunk % 3 == 2:
                tick()
        self.f2[...] += dot_back(self.hid[...], self.up[level])
        tick()
        self.norm_back(2 * level, self.f2)
        self.mix[...] = dot_back(self.xl[...], self.out[level]).astype(low)
        tick()

    def attend_back(self, tick):
        width = 2 * HEAD_DIM
        for pair in range(self.heads // 2):
            slab = slice(pair * width, (pair + 1) * width)
            query, keys, values = (self.att[i, :, slab] for i in range(3))
            grad = self.mix[:, slab]
            first = lane_half(values.shape, 0)
            grads = [], [], []
            for which in range(2):
                probs = self.probs[2 * pair + which]
                chosen = jnp.where(first == (which == 0), values, jnp.zeros_like(values))
                wide = probs.astype(f32)
                shared = wide * dot_back(chosen, grad)
                delta = jnp.sum(shared, axis=0, keepdims=True)
                dscore = (shared - wide * delta).astype(low)
                grads[0].append(dot_turned(dscore, keys))
                grads[1].append(dot(dscore, query))
                grads[2].append(dot(probs, grad))
            self.att[0, :, slab] = (jnp.where(first, *grads[0]) * HEAD_DIM**-0.5).astype(low)
            self.att[1, :, slab] = jnp.where(first, *grads[1]).astype(low)
            self.att[2, :, slab] = jnp.where(first, *grads[2]).astype(low)
            tick()

    def vectors_back(self, level, part):
        ranks = self.ranks
        total = lambda grid: jnp.sum(grid, axis=0, keepdims=True)
        sums, passed = {}, {}
        for i, (which, scale, name) in enumerate(((0, "bq", "q"), (2, "bv", "v"))):
            rows = self.att[which, part, :].astype(f32)
            sums["b" + name] = total(rows * self.lift[i, part, :].astype(f32))
            passed[name] = slice((1 + i) * ranks, (1 + i) * ranks + self.model)
            self.hid[part, passed[name]] = (rows * self.vector(scale, level)).astype(low)
        found = {"dq": [], "dv": []}
        for columns in (slice(0, ranks // 2), slice(ranks // 2, ranks)):
            inner = self.inner[part, columns].astype(f32)
            grad = 0.0
            for name in ("q", "v"):
                back = dot_back(self.hid[part, passed[name]], self.full_b[columns, :])
                found["d" + name].append(total(back * inner))
                grad += back * self.vector("d" + name, level)[:, columns]
            self.hid[part, columns] = grad.astype(low)
        sums.update({name: jnp.concatenate(pieces, axis=1) for name, pieces in found.items()})
        return sums

    def input_back(self, level, part):
        grad = self.f2[part, :] + dot_back(self.hid[part, : self.ranks], self.full_a[...])
        for i in range(3):
            grad += dot_back(self.att[i, part, :], self.qkv[level, i])
        self.x[part, :] = grad


def layers_kernel(levels, names, groups_of, *refs):
    refs = dict(zip(names, refs))
    get = refs.pop
    ins = [get(n) for n in INPUTS]
    (tokens, lengths, wq, wk, wv, wo, wu, wd, mat_a, mat_b, dq, bq, dv, bv, cotangent) = ins
    rank, batch = lax.axis_index("rank"), lax.axis_index("batch")
    both = refs["x"].shape[0]
    seq = both
    model, feat = wq.shape[1:]
    hidden, rank_part = wu.shape[2], mat_a.shape[1]
    own_x, other_x, own_g, other_g, out_sums = (get(n) for n in ("own_x", "other_x", "own_g", "other_g", "out_sums"))
    spills = [get("spill_probs"), get("spill_att"), get("spill_lift"), get("spill_inner"), get("spill_slope")]
    load_sem, spill_sem, small_send, small_recv = (get(n) for n in ("load_sem", "spill_sem", "small_send", "small_recv"))
    sems = [get(f"sem{i}") for i in range(8)]
    swap_send, swap_recv, sum_send, sum_recv = (get(n) for n in ("swap_send", "swap_recv", "sum_send", "sum_recv"))
    store_sem = get("store_sem")
    gone, came = get("gone"), get("came")
    sum_buf, sum_in, sums_ref = get("sum_buf"), get("sum_in"), get("sums")
    layers = Layers(refs)
    L = layers

    used = [0]

    def load(src, dst):
        copy = pltpu.make_async_copy(src, dst, load_sem.at[used[0]])
        used[0] += 1
        return copy

    def columns_of(size):
        return pl.ds(pl.multiple_of(rank * size, 128), size)

    def rows_of(size):
        return pl.ds(pl.multiple_of(rank * size, 16), size)

    own_rows = rows_of(seq)

    groups, loads, names_of = [], [], {}

    def add(name, found, copies):
        for i, group in enumerate(found):
            names_of[name + (str(i) if len(found) > 1 else "")] = len(groups)
            groups.append(group)
            loads.append(copies if i == 0 else [])

    add("a", [piece_rows(L.full_a, (), model, rank_part)], [load(mat_a, L.full_a.at[:, columns_of(rank_part)])])
    load_x = load(tokens.at[own_rows, :], L.xl)
    add("b", [tile_group(L.full_b, rank_part, model)], [load(mat_b, L.full_b.at[rows_of(rank_part), :])])
    for level in range(levels):
        add(f"qkv/{level}", [piece_rows(L.qkv, (level, slice(None)), model, feat)], [
            load(w.at[level], L.qkv.at[level, i, :, columns_of(feat)]) for i, w in enumerate((wq, wk, wv))])
        add(f"out/{level}", row_groups(L.out, (level,), feat, 1), [
            load(wo.at[level], L.out.at[level, rows_of(feat), :])])
        add(f"up/{level}", column_groups(L.up, (level,), model, hidden, 1), [
            load(wu.at[level], L.up.at[level, :, columns_of(hidden)])])
        add(f"down/{level}", row_groups(L.down, (level,), hidden, 1), [
            load(wd.at[level], L.down.at[level, rows_of(hidden), :])])
    vectors = [(dq, L.dq), (bq, L.bq), (dv, L.dv), (bv, L.bv)]

    small_loads = [load(src, dst.at[:, columns_of(src.shape[1])]) for src, dst in vectors]
    load_g = load(cotangent.at[own_rows, :], gone)
    exchange = Exchange(groups, loads, sems)
    for copies in (small_loads, *loads[: exchange.AHEAD], [load_x]):
        for copy in copies:
            copy.start()
    bits = (lax.axis_size("batch") - 1).bit_length()
    for bit in range(3, bits):
        exchange.partner[bit] = (flip(batch, bit), rank)
    slots = lax.broadcasted_iota(jnp.int32, L.bias.shape, 0)
    length = lengths[rank]
    L.bias[...] = jnp.where(slots < length, 0.0, masked)

    exchange.barrier()
    small = []
    for i, (src, dst) in enumerate(vectors):
        ref = dst.at[:, columns_of(src.shape[1])]
        small_loads[i].wait()
        small.append(exchange.copy(ref, ref, small_send.at[i], small_recv.at[i], "y"))
        small[-1].start()

    steps = []
    for level in range(levels):
        at = lambda name: [names_of[f"{name}/{level}"]]
        steps += [(1.3, [names_of["a"]]), (0.75, [names_of["b"]] + at("qkv")), (1.2, []), (1.2, [])]
        steps += [(0.86, [])] * (L.heads // 2) + [(1.0, at("out"))]
        steps += [(0.42, at("up") if chunk == 3 else []) for chunk in range(6)]
        steps += [(1.3, []), (1.8, at("down"))]
    exchange.plan(steps)
    load_x.wait()

    L.x[...] = L.xl[...].astype(f32)
    for copy in small:
        copy.wait()

    spill_src = [L.probs, L.att, L.lift, L.inner, L.slope]
    spill = [pltpu.make_async_copy(src, dst, spill_sem.at[i]) for i, (src, dst) in enumerate(zip(spill_src, spills))]
    fetch = [pltpu.make_async_copy(dst, src, spill_sem.at[i]) for i, (src, dst) in enumerate(zip(spill_src, spills))]
    PROBS, ATT, LIFT, INNER, SLOPE = range(5)

    for level in range(levels):
        def need(name):
            assert names_of[name if name in "ab" else f"{name}/{level}"] in exchange.here

        if level:
            for i in (ATT, LIFT, INNER, PROBS):
                spill[i].wait()
        L.adapt(level, exchange.tick, need)
        if not level:
            spill[LIFT].start()
            spill[INNER].start()
        L.attend(exchange.tick)
        if not level:
            spill[ATT].start()
            spill[PROBS].start()
        L.project(level, exchange.tick, need)
        if level:
            spill[SLOPE].wait()
        L.feed(level, rank, exchange.tick, need)
        if not level:
            spill[SLOPE].start()
    exchange.tick()
    load_g.start()

    def swap(src, index, part, slot):
        return exchange.copy(src.at[part, :], came.at[index, part], swap_send.at[index + slot],
                             swap_recv.at[index + slot], "y")

    first_rows = seq // 4
    store_own = pltpu.make_async_copy(L.x, own_x, store_sem.at[0])
    store_own.start()
    swaps = [swap(L.normed.at[2 * levels - 1], 0, pl.ds(0, seq), 0)]
    swaps[0].start()
    load_g.wait()

    def sum_copy(level, step):
        who = ["y", "c", "x", "z", *range(3, bits)][step]
        src = sum_buf.at[level, 1 - rank] if step == 0 else sum_buf.at[level, rank]
        return exchange.copy(src, sum_in.at[level, step], sum_send.at[level, step], sum_recv.at[level, step], who)

    def sum_step(level, step):
        if step:
            sum_copy(level, step - 1).wait()
            sum_buf[level, rank] += sum_in[level, step - 1]
        if step < 1 + bits:
            sum_copy(level, step).start()

    later = []

    def step_on():
        if later:
            later.pop(0)()

    ORDER = (("dq", rank_part), ("bq", feat), ("dv", rank_part), ("bv", feat))
    for level in reversed(range(levels)):
        last = level == 0
        L.feed_back(level, L.x if level < levels - 1 else gone, step_on)
        if not last:
            fetch[SLOPE].start()
        elif levels > 1:
            fetch[ATT].wait()
            fetch[PROBS].wait()
        L.attend_back(step_on)
        if not last:
            fetch[PROBS].start()
        elif levels > 1:
            fetch[LIFT].wait()
            fetch[INNER].wait()
        if level == levels - 1:
            store_own.wait()
        sums = [{}]
        parts = [pl.ds(0, seq)]
        if last:
            parts = [pl.ds(0, first_rows), pl.ds(first_rows, seq - first_rows)]
        for i, part in enumerate(parts):
            found = L.vectors_back(level, part)
            sums = {name: found[name] + sums[name] if i else found[name] for name in found}
            if i == len(parts) - 1:
                at = 0
                for name, width in ORDER:
                    for side in range(2):
                        sum_buf[level, side, :, pl.ds(at, width)] = sums[name][:, side * width : (side + 1) * width]
                    at += width
                while later:
                    step_on()
                for step in range(2 + bits):
                    later.append(functools.partial(sum_step, level, step))
                step_on()
            L.input_back(level, part)
            if last:
                gone[part, :] = L.x[part, :].astype(low)
                swaps.append(swap(gone, 1, part, i))
                swaps[-1].start()
        if not last:
            for i in (ATT, LIFT, INNER):
                fetch[i].start()
            fetch[SLOPE].wait()
    store_g = pltpu.make_async_copy(L.x, own_g, store_sem.at[1])
    store_g.start()
    exchange.settle()
    swaps[0].wait()
    store_came = [pltpu.make_async_copy(came.at[0], other_x, store_sem.at[2])]
    store_came[0].start()
    while later:
        step_on()
    for level in range(levels):
        sums_ref[level : level + 1, :] = sum_buf[level, rank]
    store_sums = pltpu.make_async_copy(sums_ref, out_sums, store_sem.at[5])
    store_sums.start()
    for i, part in enumerate(parts):
        swaps[1 + i].wait()
        store_came.append(pltpu.make_async_copy(came.at[1, part], other_g.at[part, :], store_sem.at[3 + i]))
        store_came[-1].start()
    store_g.wait()
    store_sums.wait()
    for copy in store_came:
        copy.wait()


def assemble_kernel(rank_part, feat, own_x, other_x, own_g, other_g, sums, out_x, out_g, *refs):
    out_vectors, (own, came, wide, vectors, load_sem, store_sem) = refs[:4], refs[4:]
    rank = lax.axis_index("rank")
    seq = own_x.shape[0]
    place = lambda who: pl.ds(pl.multiple_of(who * seq, 16), seq)
    loads = [pltpu.make_async_copy(sums, vectors, load_sem.at[4])]
    for i, (mine, other) in enumerate(((own_x, other_x), (own_g, other_g))):
        loads.append(pltpu.make_async_copy(other, came.at[i], load_sem.at[2 * i]))
        loads.append(pltpu.make_async_copy(mine, own.at[i], load_sem.at[2 * i + 1]))
    for copy in loads:
        copy.start()
    stores = []

    def store(src, dst):
        stores.append(pltpu.make_async_copy(src, dst, store_sem.at[len(stores)]))
        stores[-1].start()

    for i, out in enumerate((out_x, out_g)):
        loads[1 + 2 * i].wait()
        wide[i] = came[i].astype(f32)
        store(wide.at[i], out.at[place(1 - rank), :])
        loads[2 + 2 * i].wait()
        store(own.at[i], out.at[place(rank), :])
    loads[0].wait()
    at = 0
    for width, dst in zip((rank_part, feat, rank_part, feat), out_vectors):
        store(vectors.at[:, pl.ds(at, width)], dst)
        at += width
    for copy in stores:
        copy.wait()


INPUTS = ("tokens", "lengths", "wq", "wk", "wv", "wo", "wu", "wd", "mat_a", "mat_b",
          "s_dq", "s_bq", "s_dv", "s_bv", "cotangent")


def on_device(tokens, valid_len, w_query, w_key, w_value, w_out, w_up, w_down, mat_a, mat_b,
              scale_dq, scale_bq, scale_dv, scale_bv, cotangent):
    levels, model, feat = w_query.shape
    hidden, rank_part = w_up.shape[2], mat_a.shape[1]
    ranks = 2
    rows = tokens.shape[0]
    seq = rows // valid_len.shape[0]
    heads = ranks * feat // HEAD_DIM
    bits = (lax.axis_size("batch") - 1).bit_length()
    count = 4 * (2 + 4 * levels)
    shape = jax.ShapeDtypeStruct
    dma = lambda *n: pltpu.SemaphoreType.DMA(n)
    any_spec = pl.BlockSpec(memory_space=pl.ANY)
    smem_spec = pl.BlockSpec(memory_space=pltpu.SMEM)
    vmem = pltpu.VMEM
    sum_width = 2 * (rank_part + feat)
    outs = dict(
        own_x=shape((seq, model), f32),
        other_x=shape((seq, model), low),
        own_g=shape((seq, model), f32),
        other_g=shape((seq, model), low),
        out_sums=shape((levels, sum_width), f32),
        spill_probs=shape((heads, seq, seq), low),
        spill_att=shape((3, seq, model), low),
        spill_lift=shape((2, seq, model), low),
        spill_inner=shape((seq, ranks * rank_part), low),
        spill_slope=shape((seq, ranks * hidden), low),
    )
    scratch = dict(
        qkv=vmem((levels, 3, model, ranks * feat), low),
        out=vmem((levels, ranks * feat, model), low),
        up=vmem((levels, model, ranks * hidden), low),
        down=vmem((levels, ranks * hidden, model), low),
        full_a=vmem((model, ranks * rank_part), low),
        full_b=vmem((ranks * rank_part, model), low),
        dq=vmem((levels, ranks * rank_part), f32),
        bq=vmem((levels, ranks * feat), f32),
        dv=vmem((levels, ranks * rank_part), f32),
        bv=vmem((levels, ranks * feat), f32),
        bias=vmem((seq, 128), f32),
        x=vmem((seq, model), f32),
        xl=vmem((seq, model), low),
        f2=vmem((seq, model), f32),
        hid=vmem((seq, ranks * hidden), low),
        att=vmem((3, seq, model), low),
        lift=vmem((2, seq, model), low),
        inner=vmem((seq, ranks * rank_part), low),
        probs=vmem((heads, seq, seq), low),
        mix=vmem((seq, model), low),
        normed=vmem((2 * levels, seq, model), low),
        scale=vmem((2 * levels, seq, 1), f32),
        slope=vmem((seq, ranks * hidden), low),
        gone=vmem((seq, model), low),
        came=vmem((2, seq, model), low),
        sum_buf=vmem((levels, 2, 1, sum_width), f32),
        sum_in=vmem((levels, 1 + bits, 1, sum_width), f32),
        load_sem=dma(4 + 6 * levels + 6),
        spill_sem=dma(5),
        small_send=dma(4),
        small_recv=dma(4),
        swap_send=dma(4),
        swap_recv=dma(4),
        sum_send=dma(levels, 1 + bits),
        sum_recv=dma(levels, 1 + bits),
        store_sem=dma(6),
        sums=vmem((levels, sum_width), f32),
    )
    for i in range(8):
        scratch[f"sem{i}"] = dma(count if i in (1, 3, 5) else count // 4)
    names = INPUTS + tuple(outs) + tuple(scratch)
    vectors = (scale_dq, scale_bq, scale_dv, scale_bv)
    macs = seq * model * (5 * ranks * rank_part + 8 * ranks * feat + 4 * ranks * hidden) * levels
    results = pl.pallas_call(
        functools.partial(layers_kernel, levels, names, None),
        out_shape=tuple(outs.values()),
        in_specs=[any_spec, smem_spec] + [any_spec] * 13,
        out_specs=(any_spec,) * 10,
        scratch_shapes=list(scratch.values()),
        compiler_params=pltpu.CompilerParams(
            collective_id=0, has_side_effects=True, vmem_limit_bytes=64 * 2**20 - 2**18),
        cost_estimate=pl.CostEstimate(flops=2 * macs, bytes_accessed=64 * 2**20, transcendentals=0),
        name="layers",
    )(tokens, valid_len, w_query, w_key, w_value, w_out, w_up, w_down, mat_a, mat_b, *vectors, cotangent)
    return pl.pallas_call(
        functools.partial(assemble_kernel, rank_part, feat),
        out_shape=(shape((rows, model), f32),) * 2
        + tuple(shape((levels, width), f32) for width in (rank_part, feat, rank_part, feat)),
        in_specs=[pl.BlockSpec(memory_space=pltpu.HBM)] * 5,
        out_specs=(any_spec,) * 6,
        scratch_shapes=[vmem((2, seq, model), f32), vmem((2, seq, model), low), vmem((2, seq, model), f32),
                        vmem((levels, sum_width), f32), dma(5), dma(8)],
        compiler_params=pltpu.CompilerParams(vmem_limit_bytes=63 * 2**20),
        name="assemble",
    )(*results[:5])


def solution(mesh):
    split = P(None, None, "rank")
    down_split = P(None, "rank", None)
    vector = P(None, "rank")
    return jax.shard_map(
        on_device,
        mesh=mesh,
        in_specs=(P("batch", None), P("batch"), split, split, split, down_split, split, down_split,
                  P(None, "rank"), P("rank", None), vector, vector, vector, vector, P("batch", None)),
        out_specs=(P("batch", None), P("batch", None), vector, vector, vector, vector),
        check_vma=False,
    )
```
